256 devices in a mesh: user: 16 (over z_hi, y, core), item: 4 (over x), hot: 4 (over z_lo).
Axes of the slice: x: 4, y: 4, z: 8 (z_hi: 2, z_lo: 4; z = z_hi * 4 + z_lo), core: 2. Of those that a mesh axis runs over, the one named last changes fastest.
Arguments:
- user_final: float32 [32768, 256], P(('user', 'item', 'hot')), may hold values from -1.5 to 1.5
- item_final: float32 [4096, 256], P(('user', 'item', 'hot')), may hold values from -1.5 to 1.5
- tiles: float32 [12288, 128, 128], P(('user', 'item', 'hot')), may hold values from 0 to 1
- tile_rows: int32 [12288], P(('user', 'item', 'hot')), may hold values from 0 to 15, as said below
- tile_cols: int32 [12288], P(('user', 'item', 'hot')), may hold values from 0 to 7
- tile_count: int32 [256], P(('user', 'item', 'hot')), may hold values from 1 to 48, as said below
- triplets: int32 [65536, 3], P(('user', 'item', 'hot')), may hold values from 0 to 32767, as said below
Outputs:
- user_grad: float32 [32768, 256], P(('user', 'item', 'hot'))
- item_grad: float32 [4096, 256], P(('user', 'item', 'hot'))
The draws below stay inside these ranges and needn't reach their ends.
Inputs may be any that keep to these rules, and one draw needn't show every extreme that they name: `tile_count`: every device has at least one live slot; some device has exactly 1 and some exactly 48. `triplets`: rows r to r + 255 with r = d * 256 belong to device d; their users lie in that device's user block and both of their items in its item block. Column 0 holds users, columns 1 and 2 hold items. `tile_rows`: A device holds no tile position twice. Its slot s holds a tile whose row t satisfies (t // (16 / (4 * 4))) % 4 = s // (48 / 4).
All inputs are finite; a program needn't handle non-finite values.
Results may differ from the reference program's by a relative error of at most 0.0003.
Values sent between devices are 32-bit elements; how exact they have to be, the bound alone decides.
A program may use at most 64 MiB of HBM per device.

```python
import jax
import jax.numpy as jnp
from jax import lax

D = 256
TILE = 128
LAYERS = 2
UT = 16
IT = 8
SLOTS = 48
BATCH = 256
USERS = 32768
ITEMS = 4096
N_USER = 16
N_ITEM = 4
N_HOT = 4


def slot_places(key):
    device_total = N_USER * N_ITEM * N_HOT
    group_slots = SLOTS // N_HOT
    class_places = UT * IT // N_HOT
    row_span = UT // (N_ITEM * N_HOT)
    keys = jax.random.split(key, device_total * N_HOT)
    picks = jax.vmap(lambda single: jax.random.permutation(single, class_places)[:group_slots])(keys)
    picks = picks.reshape(device_total, N_HOT, group_slots)
    group = jnp.arange(N_HOT, dtype=jnp.int32)[None, :, None]
    class_row = picks // IT
    rows = class_row // row_span * row_span * N_HOT + group * row_span + class_row % row_span
    cols = picks % IT
    return (rows.reshape(-1).astype(jnp.int32), cols.reshape(-1).astype(jnp.int32))


def draw_tile_rows(key, part):
    rows, cols = slot_places(key)
    return rows


def draw_tile_cols(key, part):
    rows, cols = slot_places(key)
    return cols


def draw_tiles(key, part):
    key = jax.random.fold_in(key, 31)
    fan = N_HOT * SLOTS * TILE * max(N_USER, N_ITEM) // UT
    top = (3.0 / fan) ** 0.5
    shape = (SLOTS * N_USER * N_ITEM * N_HOT, TILE, TILE)
    return jax.random.uniform(key, shape, jnp.float32, 0.0, top)


def draw_tile_count(key, part):
    key = jax.random.fold_in(key, 11)
    device_total = N_USER * N_ITEM * N_HOT
    first_key, second_key, third_key = jax.random.split(key, 3)
    counts = jax.random.randint(first_key, (device_total,), 1, SLOTS + 1)
    full_device = jax.random.randint(second_key, (), 0, device_total)
    single_device = (full_device + 1 + jax.random.randint(third_key, (), 0, device_total - 1)) % device_total
    places = jnp.arange(device_total)
    counts = jnp.where(places == full_device, SLOTS, jnp.where(places == single_device, 1, counts))
    return counts.astype(jnp.int32)


def draw_triplets(key, part):
    key = jax.random.fold_in(key, 23)
    device_total = N_USER * N_ITEM * N_HOT
    row_total = device_total * BATCH
    block_users = UT * TILE
    block_items = IT * TILE
    item_share = block_items // (N_USER * N_HOT)
    row_index = jnp.arange(row_total, dtype=jnp.int32)
    device_of = row_index // BATCH
    user_block = device_of // (N_ITEM * N_HOT)
    item_block = device_of // N_HOT % N_ITEM
    first_key, second_key, third_key = jax.random.split(key, 3)
    first_row = row_index == 0
    last_row = row_index == row_total - 1
    buyer_local = jax.random.randint(first_key, (row_total,), 0, block_users)
    buyer_local = jnp.where(first_row, 0, jnp.where(last_row, block_users - 1, buyer_local))
    buyers = user_block * block_users + buyer_local

    def place(local_row):
        outer_part = local_row // (N_HOT * item_share)
        hot_part = local_row // item_share % N_HOT
        inner_part = local_row % item_share
        return ((outer_part * N_ITEM + item_block) * N_HOT + hot_part) * item_share + inner_part
    chosen_local = jax.random.randint(second_key, (row_total,), 0, block_items)
    chosen_local = jnp.where(last_row, block_items - 1, chosen_local)
    others_local = jax.random.randint(third_key, (row_total,), 0, block_items)
    others_local = jnp.where(first_row, 0, others_local)
    chosen = place(chosen_local)
    others = place(others_local)
    return jnp.stack([buyers, chosen, others], axis=1).astype(jnp.int32)


def block_scale(stream_key, extent, pieces, smallest, top_value):
    def one(dim, blocks):
        heights = jax.random.uniform(jax.random.fold_in(jax.random.fold_in(stream_key, 6), dim), (blocks,), jnp.float32, smallest / len(pieces), top_value / len(pieces))
        return jnp.repeat(jnp.exp(heights), extent[dim] // blocks).reshape((-1,) + (1,) * (len(extent) - dim - 1))

    gain = one(*pieces[0])
    for cut in pieces[1:]:
        gain = gain * one(*cut)
    return gain


def bell_draw(own_key, dims, deviation, most, shards=(), held_as=jnp.bfloat16):
    factor_of = block_scale(own_key, dims, shards, -0.22, 0.18) if shards else 1.0
    result = jax.random.normal(own_key, dims, jnp.float32) * deviation * factor_of
    return jnp.minimum(jnp.maximum(result, -most), most).astype(held_as)


def setup_inputs(seed: int = 0) -> dict:
    seeds = jax.random.split(jax.random.key(seed), 8)
    user_final = bell_draw(seeds[0], (USERS, D), 0.25, 1.5, ((0, 256),), jnp.float32)
    item_final = bell_draw(seeds[1], (ITEMS, D), 0.25, 1.5, ((0, 256),), jnp.float32)
    tiles = draw_tiles(jax.random.fold_in(seeds[7], 71), 0)
    tile_rows = draw_tile_rows(jax.random.fold_in(seeds[7], 71), 0)
    tile_cols = draw_tile_cols(jax.random.fold_in(seeds[7], 71), 0)
    tile_count = draw_tile_count(jax.random.fold_in(seeds[7], 71), 0)
    triplets = draw_triplets(jax.random.fold_in(seeds[7], 71), 0)
    return {"user_final": user_final, "item_final": item_final, "tiles": tiles, "tile_rows": tile_rows, "tile_cols": tile_cols, "tile_count": tile_count, "triplets": triplets}


def reference(user_final, item_final, tiles, tile_rows, tile_cols, tile_count, triplets):
    block_users = UT * TILE
    block_items = IT * TILE
    item_share = block_items // (N_USER * N_HOT)
    width = user_final.shape[1]
    highest = lax.Precision.HIGHEST
    device_total = N_USER * N_ITEM * N_HOT

    def item_blocks(field):
        shaped = field.reshape(N_USER, N_ITEM, N_HOT * item_share, width)
        return shaped.transpose(1, 0, 2, 3).reshape(N_ITEM, block_items, width)

    def item_unblock(field):
        shaped = field.reshape(N_ITEM, N_USER, N_HOT * item_share, width)
        return shaped.transpose(1, 0, 2, 3).reshape(N_ITEM * block_items, width)

    buyers = triplets[:, 0]
    chosen = triplets[:, 1]
    others = triplets[:, 2]
    buyer_rows = user_final[buyers]
    chosen_rows = item_final[chosen]
    other_rows = item_final[others]
    margin = jnp.sum(buyer_rows * (chosen_rows - other_rows), axis=1)
    weight_t = -jax.nn.sigmoid(-margin)
    grad_users = jnp.zeros(user_final.shape, jnp.float32).at[buyers].add(weight_t[:, None] * (chosen_rows - other_rows))
    grad_items = jnp.zeros(item_final.shape, jnp.float32).at[chosen].add(weight_t[:, None] * buyer_rows)
    grad_items = grad_items.at[others].add(-weight_t[:, None] * buyer_rows)
    grad_items = item_blocks(grad_items)

    tile_stack = tiles.reshape(device_total, SLOTS, TILE, TILE)
    alive = (jnp.arange(SLOTS, dtype=jnp.int32)[None, :] < tile_count[:, None]).astype(jnp.float32)
    row_stack = tile_rows.reshape(device_total, SLOTS)
    col_stack = tile_cols.reshape(device_total, SLOTS)

    def propagate(user_field, item_blocked):
        user_tiles = user_field.reshape(N_USER, UT, TILE, width)
        item_tiles = item_blocked.reshape(N_ITEM, IT, TILE, width)

        def visit(carry, device):
            to_users, to_items = carry
            user_block = device // (N_ITEM * N_HOT)
            item_block = (device // N_HOT) % N_ITEM
            masked = tile_stack[device] * alive[device][:, None, None]
            rows_here = row_stack[device]
            cols_here = col_stack[device]
            item_part = item_tiles[item_block][cols_here]
            user_part = user_tiles[user_block][rows_here]
            to_users = to_users.at[user_block, rows_here].add(
                jnp.einsum('str,srd->std', masked, item_part, precision=highest))
            to_items = to_items.at[item_block, cols_here].add(
                jnp.einsum('str,std->srd', masked, user_part, precision=highest))
            return (to_users, to_items), None

        start = (jnp.zeros(user_tiles.shape, jnp.float32), jnp.zeros(item_tiles.shape, jnp.float32))
        (to_users, to_items), _ = lax.scan(visit, start, jnp.arange(device_total, dtype=jnp.int32))
        return to_users.reshape(user_field.shape), to_items.reshape(item_blocked.shape)

    state_users = grad_users
    state_items = grad_items
    for section_index in range(LAYERS):
        from_items, from_users = propagate(state_users, state_items)
        state_users = grad_users + from_items
        state_items = grad_items + from_users
    return state_users / (LAYERS + 1.0), item_unblock(state_items) / (LAYERS + 1.0)
```

```python
import jax
import jax.numpy as jnp
from jax import lax
from jax.experimental import pallas as pl
from jax.experimental.pallas import tpu as pltpu
from jax.sharding import PartitionSpec as P

MESH = pl.DeviceIdType.MESH
F32 = jnp.float32
BF16 = jnp.bfloat16
LAYERS = 2
ROUNDS = LAYERS + 1
GROUP = 12
PLACES = 32

U_AG, Z_AG, Y_AG, C_AG, C_RS, Y_RS, Z_RS, U_RS = 0, 3, 10, 13, 17, 21, 24, 31
PER_ROUND = 34
INTS = PER_ROUND * ROUNDS
TILES = INTS + 3
COPIES = TILES + 3


def split2(x):
    hi = x.astype(BF16)
    return hi, (x - hi.astype(F32)).astype(BF16)


def split3(x):
    hi = x.astype(BF16)
    rest = x - hi.astype(F32)
    mid = rest.astype(BF16)
    return hi, mid, (rest - mid.astype(F32)).astype(BF16)


def dot(a, b):
    return jnp.dot(a, b, preferred_element_type=F32)


def dot_nt(a, b):
    return lax.dot_general(a, b, (((1,), (1,)), ((), ())), preferred_element_type=F32)


def kernel(
    ints_ref,
    uf_ref,
    if_ref,
    tiles_ref,
    uo_ref,
    io_ref,
    gints,
    sints,
    tbuf,
    ah,
    al,
    ath,
    atl,
    ohu,
    ohd,
    ut,
    dt,
    wd,
    wu,
    ub,
    ib,
    pu,
    pi,
    um,
    ua,
    uz,
    rc,
    hb,
    ym,
    ya,
    yz,
    zs,
    zb,
    gu,
    gi,
    ssem,
    rsem,
    lsem,
):
    a = lax.axis_index("user")
    b = lax.axis_index("item")
    c = lax.axis_index("hot")
    core = a % 2
    y = (a // 2) % 4
    zhi = a // 8
    z = zhi * 4 + c

    def user_index(zhi_, y_, core_):
        return (zhi_ * 4 + y_) * 2 + core_

    def ring(v):
        even = v + 1 - 2 * (v % 2)
        odd = 3 - v
        first = (1 - core) * even + core * odd
        second = (1 - core) * odd + core * even
        return first, second, (v + 2) % 4

    x1, x2, xo = ring(b)
    y1, y2, yo = ring(y)
    ya_dev = (user_index(zhi, y1, core), b, c)
    yb_dev = (user_index(zhi, y2, core), b, c)
    xa_dev = (a, x1, c)
    xb_dev = (a, x2, c)
    sib = (user_index(zhi, y, 1 - core), b, c)

    def z_dev(k):
        other = (z + k) % 8
        return (user_index(other // 4, y, core), b, other % 4), other // 4, other % 4

    def hot_dev(k):
        other = (c + k) % 4
        return (a, b, other), other

    started = []

    def send(src, dst, index, dev):
        copy = pltpu.make_async_remote_copy(
            src_ref=src,
            dst_ref=dst,
            send_sem=ssem.at[index],
            recv_sem=rsem.at[index],
            device_id=dev,
            device_id_type=MESH,
        )
        copy.start()
        started.append(copy)

    def arrive(dst, index, dev):
        pltpu.make_async_remote_copy(
            src_ref=dst,
            dst_ref=dst,
            send_sem=ssem.at[index],
            recv_sem=rsem.at[index],
            device_id=dev,
            device_id_type=MESH,
        ).wait_recv()

    barrier = pltpu.get_barrier_semaphore()
    peers = [xa_dev, xb_dev, ya_dev, yb_dev, sib] + [z_dev(k)[0] for k in range(1, 8)]
    for dev in peers:
        pl.semaphore_signal(barrier, inc=1, device_id=dev, device_id_type=MESH)
    own_tiles = pltpu.make_async_copy(
        tiles_ref.at[pl.ds(c * GROUP, GROUP)], tbuf.at[c, pl.ds(0, GROUP)], lsem.at[0]
    )
    own_tiles.start()
    for h in range(4):
        tbuf[h, GROUP] = jnp.zeros((128, 128), F32)
    gints[c] = ints_ref[...]
    pl.semaphore_wait(barrier, len(peers))

    def gather_start(r, users, items):
        base = r * PER_ROUND
        ub[r, b] = users
        ib[r, zhi, y, core, pl.ds(pl.multiple_of(c * 16, 16), 16)] = items
        mine = ib.at[r, zhi, y, core, pl.ds(pl.multiple_of(c * 16, 16), 16)]
        for k in range(1, 8):
            send(mine, mine, base + Z_AG + k - 1, z_dev(k)[0])
        send(ub.at[r, b], ub.at[r, b], base + U_AG, xa_dev)
        send(ub.at[r, b], ub.at[r, b], base + U_AG + 1, xb_dev)

    def gather_users_forward(r):
        base = r * PER_ROUND
        arrive(ub.at[r, x1], base + U_AG, xa_dev)
        send(ub.at[r, x1], ub.at[r, x1], base + U_AG + 2, xb_dev)

    def gather_items_z(r):
        base = r * PER_ROUND
        for k in range(1, 8):
            dev, other_hi, other_lo = z_dev(8 - k)
            piece = ib.at[r, other_hi, y, core, pl.ds(pl.multiple_of(other_lo * 16, 16), 16)]
            arrive(piece, base + Z_AG + k - 1, dev)
        piece = ib.at[r, :, y, core]
        send(piece, piece, base + Y_AG, ya_dev)
        send(piece, piece, base + Y_AG + 1, yb_dev)
        send(piece, piece, base + C_AG, sib)

    def gather_items_y(r):
        base = r * PER_ROUND
        first = ib.at[r, :, y1, core]
        arrive(first, base + Y_AG, ya_dev)
        send(first, first, base + Y_AG + 2, yb_dev)
        send(first, first, base + C_AG + 1 + 2 * core, sib)
        second = ib.at[r, :, y2, core]
        arrive(second, base + Y_AG + 1, yb_dev)
        send(second, second, base + C_AG + 3 - 2 * core, sib)
        far = ib.at[r, :, yo, core]
        arrive(far, base + Y_AG + 2, yb_dev)
        send(far, far, base + C_AG + 2, sib)

    def gather_users_end(r):
        base = r * PER_ROUND
        arrive(ub.at[r, x2], base + U_AG + 1, xb_dev)
        arrive(ub.at[r, xo], base + U_AG + 2, xb_dev)

    def gather_items_end(r):
        base = r * PER_ROUND
        for k, other in ((0, y), (1, y + 1 - 2 * (y % 2)), (3, 3 - y), (2, yo)):
            arrive(ib.at[r, :, other, 1 - core], base + C_AG + k, sib)

    def scatter_items_core(r):
        base = r * PER_ROUND
        for k, other in ((2, yo), (1, y + 1 - 2 * (y % 2)), (3, 3 - y), (0, y)):
            send(pi.at[r, :, other, 1 - core], rc.at[r, :, other], base + C_RS + k, sib)

    def scatter_users_start(r):
        base = r * PER_ROUND
        send(pu.at[r, xo], um.at[r], base + U_RS, xb_dev)
        send(pu.at[r, x2], uz.at[r], base + U_RS + 1, xb_dev)

    def scatter_items_y(r):
        base = r * PER_ROUND

        def halves(k, other):
            arrive(rc.at[r, :, other], base + C_RS + k, sib)
            hb[r, other] = pi[r, :, other, core] + rc[r, :, other]

        halves(2, yo)
        send(hb.at[r, yo], ym.at[r], base + Y_RS, yb_dev)
        halves(1, y + 1 - 2 * (y % 2))
        halves(3, 3 - y)
        send(hb.at[r, y2], yz.at[r], base + Y_RS + 1, yb_dev)
        halves(0, y)

    def scatter_users_forward(r):
        base = r * PER_ROUND
        arrive(um.at[r], base + U_RS, xb_dev)
        pu[r, x1] = pu[r, x1] + um[r]
        send(pu.at[r, x1], ua.at[r], base + U_RS + 2, xa_dev)

    def scatter_items_z(r):
        base = r * PER_ROUND
        arrive(ym.at[r], base + Y_RS, yb_dev)
        hb[r, y1] = hb[r, y1] + ym[r]
        send(hb.at[r, y1], ya.at[r], base + Y_RS + 2, ya_dev)
        arrive(yz.at[r], base + Y_RS + 1, yb_dev)
        arrive(ya.at[r], base + Y_RS + 2, ya_dev)
        zs[r] = hb[r, y] + yz[r] + ya[r]
        for k in range(1, 8):
            dev, other_hi, other_lo = z_dev(k)
            send(
                zs.at[r, other_hi, pl.ds(pl.multiple_of(other_lo * 16, 16), 16)],
                zb.at[r, k - 1],
                base + Z_RS + k - 1,
                dev,
            )

    def scatter_users_end(r):
        base = r * PER_ROUND
        arrive(uz.at[r], base + U_RS + 1, xb_dev)
        arrive(ua.at[r], base + U_RS + 2, xa_dev)
        return pu[r, b] + uz[r] + ua[r]

    def scatter_items_end(r):
        base = r * PER_ROUND
        total = zs[r, zhi, pl.ds(pl.multiple_of(c * 16, 16), 16)]
        for k in range(1, 8):
            arrive(zb.at[r, k - 1], base + Z_RS + k - 1, z_dev(8 - k)[0])
            total = total + zb[r, k - 1]
        return total

    def store_items(r, m, value):
        first = 2 * m % 4
        pi[r, m // 2, first : first + 2] = value.reshape(2, 2, 64, 256)

    def scatter(r):
        scatter_items_y(r)
        scatter_users_forward(r)
        scatter_items_z(r)
        users = scatter_users_end(r)
        items = scatter_items_end(r)
        return users, items

    gather_start(0, uf_ref[...], if_ref[...])
    for k in range(1, 4):
        dev, other = hot_dev(k)
        send(gints.at[c], gints.at[c], INTS + k - 1, dev)
    for k in range(1, 4):
        dev, other = hot_dev(k)
        send(
            tiles_ref.at[pl.ds(other * GROUP, GROUP)],
            tbuf.at[c, pl.ds(0, GROUP)],
            TILES + k - 1,
            dev,
        )
    gather_users_forward(0)
    gather_items_z(0)
    for k in range(1, 4):
        dev, other = hot_dev(4 - k)
        arrive(gints.at[other], INTS + k - 1, dev)
    to_scalars = pltpu.make_async_copy(gints, sints, lsem.at[1])
    to_scalars.start()
    for h in range(4):
        span = slice(h * 256, (h + 1) * 256)
        buyers = jnp.where(gints[h, 1:2, :] == c, gints[h, 0:1, :], -1)
        rows = lax.broadcasted_iota(jnp.int32, (512, 256), 0)
        ohu[:, span] = jnp.where(rows == buyers, 1.0, 0.0).astype(BF16)
        rows = lax.broadcasted_iota(jnp.int32, (1024, 256), 0)
        chosen = jnp.where(rows == gints[h, 2:3, :], 1.0, 0.0)
        others = jnp.where(rows == gints[h, 3:4, :], 1.0, 0.0)
        ohd[:, span] = (chosen - others).astype(BF16)
    gather_items_y(0)
    gather_users_end(0)
    ut[0], ut[1], ut[2] = split3(ub[0].reshape(512, 256).T)
    gather_items_end(0)
    dt[0], dt[1], dt[2] = split3(ib[0].reshape(1024, 256).T)
    for h in range(4):
        span = slice(h * 256, (h + 1) * 256)
        buyer = dot(ut[0], ohu[:, span]) + dot(ut[1], ohu[:, span]) + dot(ut[2], ohu[:, span])
        differ = dot(dt[0], ohd[:, span]) + dot(dt[1], ohd[:, span]) + dot(dt[2], ohd[:, span])
        margin = jnp.sum(buyer * differ, axis=0, keepdims=True)
        small = jnp.exp(-jnp.abs(margin))
        coef = -jnp.where(margin >= 0, small, 1.0) / (1.0 + small)
        wu[0, :, span], wu[1, :, span] = split2(coef * buyer)
        wd[0, :, span], wd[1, :, span] = split2(coef * differ)
    for m in range(4):
        left = ohd[m * 256 : (m + 1) * 256, :]
        store_items(0, m, dot_nt(left, wu[0]) + dot_nt(left, wu[1]))
    scatter_items_core(0)
    pu[0] = (dot_nt(ohu[...], wd[0]) + dot_nt(ohu[...], wd[1])).reshape(4, 128, 256)
    scatter_users_start(0)
    users, items = scatter(0)
    gu[...] = users
    gi[...] = items

    for r in range(1, ROUNDS):
        gather_start(r, users, items)
        gather_users_forward(r)
        gather_items_z(r)
        gather_items_y(r)
        if r == 1:
            to_scalars.wait()
            own_tiles.wait()
            for k in range(1, 4):
                dev, other = hot_dev(4 - k)
                arrive(tbuf.at[other, pl.ds(0, GROUP)], TILES + k - 1, dev)

            def place(row, carry):
                at_row = pl.ds(pl.multiple_of(row * 128, 128), 128)
                for col in range(8):
                    at_col = slice(col * 128, (col + 1) * 128)
                    spot = c * PLACES + row * 8 + col
                    tile = tbuf[0, sints[0, 4, spot]]
                    for h in range(1, 4):
                        tile = tile + tbuf[h, sints[h, 4, spot]]
                    ah[at_row, at_col], al[at_row, at_col] = split2(tile)
                    ath[at_col, at_row], atl[at_col, at_row] = split2(tile.T)
                return carry

            lax.fori_loop(0, 4, place, 0)
        gather_users_end(r)
        uh, ul = split2(ub[r].reshape(512, 256))
        for m in range(4):
            rows = slice(m * 256, (m + 1) * 256)
            store_items(r, m, dot(ath[rows], uh) + dot(ath[rows], ul) + dot(atl[rows], uh))
        scatter_items_core(r)
        gather_items_end(r)
        xh, xl = split2(ib[r].reshape(1024, 256))
        pu[r] = (dot(ah[...], xh) + dot(ah[...], xl) + dot(al[...], xh)).reshape(4, 128, 256)
        scatter_users_start(r)
        users, items = scatter(r)
        users = gu[...] + users
        items = gi[...] + items

    uo_ref[...] = users / (LAYERS + 1.0)
    io_ref[...] = items / (LAYERS + 1.0)
    for copy in started:
        copy.wait_send()


def body(user_final, item_final, tiles, tile_rows, tile_cols, tile_count, triplets):
    slots = tiles.shape[0]
    buyers = triplets[:, 0] % 2048
    chosen = triplets[:, 1] // 256 * 64 + triplets[:, 1] % 64
    others = triplets[:, 2] // 256 * 64 + triplets[:, 2] % 64
    slot = jnp.arange(slots, dtype=jnp.int32)
    spot = slot // GROUP * PLACES + tile_rows // 4 * 8 + tile_cols
    spot = jnp.where(slot < tile_count[0], spot, -1)
    match = spot[None, :] == jnp.arange(4 * PLACES, dtype=jnp.int32)[:, None]
    source = GROUP + jnp.sum(jnp.where(match, slot % GROUP - GROUP, 0), axis=1)
    source = jnp.concatenate([source, source])
    blank = jnp.zeros_like(source)
    ints = jnp.stack(
        [
            buyers // 512 * 128 + buyers % 128,
            buyers // 128 % 4,
            chosen,
            others,
            source,
            blank,
            blank,
            blank,
        ]
    ).astype(jnp.int32)
    vmem = pl.BlockSpec(memory_space=pltpu.VMEM)
    return pl.pallas_call(
        kernel,
        out_shape=(
            jax.ShapeDtypeStruct((128, 256), F32),
            jax.ShapeDtypeStruct((16, 256), F32),
        ),
        in_specs=[vmem, vmem, vmem, pl.BlockSpec(memory_space=pl.ANY)],
        out_specs=(vmem, vmem),
        scratch_shapes=[
            pltpu.VMEM((4, 8, 256), jnp.int32),
            pltpu.SMEM((4, 8, 256), jnp.int32),
            pltpu.VMEM((4, GROUP + 1, 128, 128), F32),
            pltpu.VMEM((512, 1024), BF16),
            pltpu.VMEM((512, 1024), BF16),
            pltpu.VMEM((1024, 512), BF16),
            pltpu.VMEM((1024, 512), BF16),
            pltpu.VMEM((512, 1024), BF16),
            pltpu.VMEM((1024, 1024), BF16),
            pltpu.VMEM((3, 256, 512), BF16),
            pltpu.VMEM((3, 256, 1024), BF16),
            pltpu.VMEM((2, 256, 1024), BF16),
            pltpu.VMEM((2, 256, 1024), BF16),
            pltpu.VMEM((ROUNDS, 4, 128, 256), F32),
            pltpu.VMEM((ROUNDS, 2, 4, 2, 64, 256), F32),
            pltpu.VMEM((ROUNDS, 4, 128, 256), F32),
            pltpu.VMEM((ROUNDS, 2, 4, 2, 64, 256), F32),
            pltpu.VMEM((ROUNDS, 128, 256), F32),
            pltpu.VMEM((ROUNDS, 128, 256), F32),
            pltpu.VMEM((ROUNDS, 128, 256), F32),
            pltpu.VMEM((ROUNDS, 2, 4, 64, 256), F32),
            pltpu.VMEM((ROUNDS, 4, 2, 64, 256), F32),
            pltpu.VMEM((ROUNDS, 2, 64, 256), F32),
            pltpu.VMEM((ROUNDS, 2, 64, 256), F32),
            pltpu.VMEM((ROUNDS, 2, 64, 256), F32),
            pltpu.VMEM((ROUNDS, 2, 64, 256), F32),
            pltpu.VMEM((ROUNDS, 7, 16, 256), F32),
            pltpu.VMEM((128, 256), F32),
            pltpu.VMEM((16, 256), F32),
            pltpu.SemaphoreType.DMA((COPIES,)),
            pltpu.SemaphoreType.DMA((COPIES,)),
            pltpu.SemaphoreType.DMA((2,)),
        ],
        compiler_params=pltpu.CompilerParams(
            collective_id=0, has_side_effects=True, vmem_limit_bytes=52 * 1024 * 1024
        ),
        name="propagate",
    )(ints, user_final, item_final, tiles)


def solution(mesh):
    placed = (
        P(("user", "item", "hot"), None),
        P(("user", "item", "hot"), None),
        P(("user", "item", "hot"), None, None),
        P(("user", "item", "hot")),
        P(("user", "item", "hot")),
        P(("user", "item", "hot")),
        P(("user", "item", "hot"), None),
    )
    return jax.shard_map(
        body,
        mesh=mesh,
        in_specs=placed,
        out_specs=(P(("user", "item", "hot"), None), P(("user", "item", "hot"), None)),
        check_vma=False,
    )
```

```python
import jax
import jax.numpy as jnp
from jax import lax
from jax.experimental import pallas as pl
from jax.experimental.pallas import tpu as pltpu
from jax.sharding import PartitionSpec as P

MESH = pl.DeviceIdType.MESH
F32 = jnp.float32
BF16 = jnp.bfloat16
LAYERS = 2


ROUNDS = LAYERS + 1
GROUP = 12
PLACES = 32

U_AG, Z_AG, Y_AG, C_AG, C_RS, Y_RS, Z_RS, U_RS = 0, 7, 14, 17, 21, 25, 28, 35
PER_ROUND = 42
INTS = PER_ROUND * ROUNDS
TILES = INTS + 3
COPIES = TILES + 2


def split2(x):
    hi = x.astype(BF16)
    return hi, (x - hi.astype(F32)).astype(BF16)


def split3(x):
    hi = x.astype(BF16)
    rest = x - hi.astype(F32)
    mid = rest.astype(BF16)
    return hi, mid, (rest - mid.astype(F32)).astype(BF16)


def dot(a, b):
    return jnp.dot(a, b, preferred_element_type=F32)


def dot_nt(a, b):
    return lax.dot_general(a, b, (((1,), (1,)), ((), ())), preferred_element_type=F32)


def kernel(
    ints_ref,
    uf_ref,
    if_ref,
    tiles_ref,
    uo_ref,
    io_ref,
    gints,
    sints,
    tbuf0,
    tbuf1,
    ah,
    al,
    ath,
    atl,
    ohu,
    ohd,
    ut,
    dt,
    wd,
    wu,
    ub,
    ib,
    pu,
    pi,
    um,
    ua,
    uz,
    uq,
    rc,
    hb,
    ym,
    ya,
    yz,
    zs,
    zb,
    gu,
    gi,
    ssem,
    rsem,
    lsem,
):
    a = lax.axis_index("user")
    b = lax.axis_index("item")
    c = lax.axis_index("hot")
    core = a % 2
    y = (a // 2) % 4
    zhi = a // 8
    z = zhi * 4 + c

    def user_index(zhi_, y_, core_):
        return (zhi_ * 4 + y_) * 2 + core_

    def ring(v):
        even = v + 1 - 2 * (v % 2)
        odd = 3 - v
        first = (1 - core) * even + core * odd
        second = (1 - core) * odd + core * even
        return first, second, (v + 2) % 4

    x1, x2, xo = ring(b)
    y1, y2, yo = ring(y)
    ya_dev = (user_index(zhi, y1, core), b, c)
    yb_dev = (user_index(zhi, y2, core), b, c)
    xa_dev = (a, x1, c)
    xb_dev = (a, x2, c)
    tbuf = (tbuf0, tbuf1)
    slot = c // 2
    pair = c + 1 - 2 * (c % 2)
    pair_dev = (a, b, pair)
    far_dev = (a, b, (c + 2) % 4)
    sib = (user_index(zhi, y, 1 - core), b, c)

    def z_dev(k):
        other = (z + k) % 8
        return (user_index(other // 4, y, core), b, other % 4), other // 4, other % 4

    def hot_dev(k):
        other = (c + k) % 4
        return (a, b, other), other

    started = []

    def send(src, dst, index, dev):
        copy = pltpu.make_async_remote_copy(
            src_ref=src,
            dst_ref=dst,
            send_sem=ssem.at[index],
            recv_sem=rsem.at[index],
            device_id=dev,
            device_id_type=MESH,
        )
        copy.start()
        started.append(copy)

    def arrive(dst, index, dev):
        pltpu.make_async_remote_copy(
            src_ref=dst,
            dst_ref=dst,
            send_sem=ssem.at[index],
            recv_sem=rsem.at[index],
            device_id=dev,
            device_id_type=MESH,
        ).wait_recv()

    barrier = pltpu.get_barrier_semaphore()
    peers = [xa_dev, xb_dev, ya_dev, yb_dev, sib] + [z_dev(k)[0] for k in range(1, 8)]
    for dev in peers:
        pl.semaphore_signal(barrier, inc=1, device_id=dev, device_id_type=MESH)
    own_tiles = [
        pltpu.make_async_copy(
            tiles_ref.at[pl.ds((2 * h + c % 2) * GROUP, GROUP)],
            tbuf[h].at[0, pl.ds(0, GROUP)],
            lsem.at[h],
        )
        for h in range(2)
    ]
    for copy in own_tiles:
        copy.start()
    for h in range(2):
        tbuf[h][0, GROUP] = jnp.zeros((128, 128), F32)
        tbuf[h][1, GROUP] = jnp.zeros((128, 128), F32)
    gints[c] = ints_ref[...]
    pl.semaphore_wait(barrier, len(peers))

    def gather_start(r, users, items):
        base = r * PER_ROUND
        ib[r, zhi, y, core, pl.ds(pl.multiple_of(c * 16, 16), 16)] = items
        mine = ib.at[r, zhi, y, core, pl.ds(pl.multiple_of(c * 16, 16), 16)]
        for k in range(1, 8):
            send(mine, mine, base + Z_AG + k - 1, z_dev(k)[0])
        ub[r, slot, b] = users
        mine = ub.at[r, slot, b]
        if r:
            send(mine, mine, base + U_AG + 6, far_dev)
        send(mine, mine, base + U_AG, xa_dev)
        send(mine, mine, base + U_AG + 1, xb_dev)

    def gather_users_far(r):
        base = r * PER_ROUND + U_AG
        other = ub.at[r, 1 - slot, b]
        arrive(other, base + 6, far_dev)
        send(other, other, base + 3, xa_dev)
        send(other, other, base + 4, xb_dev)

    def gather_users_forward(r, own):
        base = r * PER_ROUND + U_AG + (0 if own else 3)
        block = ub.at[r, slot if own else 1 - slot, x1]
        arrive(block, base, xa_dev)
        send(block, block, base + 2, xb_dev)

    def gather_items_z(r):
        base = r * PER_ROUND
        for k in range(1, 8):
            dev, other_hi, other_lo = z_dev(8 - k)
            piece = ib.at[r, other_hi, y, core, pl.ds(pl.multiple_of(other_lo * 16, 16), 16)]
            arrive(piece, base + Z_AG + k - 1, dev)
        piece = ib.at[r, :, y, core]
        send(piece, piece, base + Y_AG, ya_dev)
        send(piece, piece, base + Y_AG + 1, yb_dev)
        send(piece, piece, base + C_AG, sib)

    def gather_items_y(r):
        base = r * PER_ROUND
        first = ib.at[r, :, y1, core]
        arrive(first, base + Y_AG, ya_dev)
        send(first, first, base + Y_AG + 2, yb_dev)
        send(first, first, base + C_AG + 1 + 2 * core, sib)
        second = ib.at[r, :, y2, core]
        arrive(second, base + Y_AG + 1, yb_dev)
        send(second, second, base + C_AG + 3 - 2 * core, sib)
        far = ib.at[r, :, yo, core]
        arrive(far, base + Y_AG + 2, yb_dev)
        send(far, far, base + C_AG + 2, sib)

    def gather_users_end(r, own):
        base = r * PER_ROUND + U_AG + (0 if own else 3)
        place = slot if own else 1 - slot
        arrive(ub.at[r, place, x2], base + 1, xb_dev)
        arrive(ub.at[r, place, xo], base + 2, xb_dev)

    def gather_items_end(r):
        base = r * PER_ROUND
        for k, other in ((0, y), (1, y + 1 - 2 * (y % 2)), (3, 3 - y), (2, yo)):
            arrive(ib.at[r, :, other, 1 - core], base + C_AG + k, sib)

    def scatter_items_core(r):
        base = r * PER_ROUND
        for k, other in ((2, yo), (1, y + 1 - 2 * (y % 2)), (3, 3 - y), (0, y)):
            send(pi.at[r, :, other, 1 - core], rc.at[r, :, other], base + C_RS + k, sib)

    def scatter_users_start(r, own):
        base = r * PER_ROUND + U_RS + 3 * own
        place = slot if own else 1 - slot
        send(pu.at[r, place, xo], um.at[r, own], base, xb_dev)
        send(pu.at[r, place, x2], uz.at[r, own], base + 1, xb_dev)

    def scatter_items_y(r):
        base = r * PER_ROUND

        def halves(k, other):
            arrive(rc.at[r, :, other], base + C_RS + k, sib)
            hb[r, other] = pi[r, :, other, core] + rc[r, :, other]

        halves(2, yo)
        send(hb.at[r, yo], ym.at[r], base + Y_RS, yb_dev)
        halves(1, y + 1 - 2 * (y % 2))
        halves(3, 3 - y)
        send(hb.at[r, y2], yz.at[r], base + Y_RS + 1, yb_dev)
        halves(0, y)

    def scatter_users_forward(r, own):
        base = r * PER_ROUND + U_RS + 3 * own
        place = slot if own else 1 - slot
        arrive(um.at[r, own], base, xb_dev)
        pu[r, place, x1] = pu[r, place, x1] + um[r, own]
        send(pu.at[r, place, x1], ua.at[r, own], base + 2, xa_dev)

    def scatter_items_z(r):
        base = r * PER_ROUND
        arrive(ym.at[r], base + Y_RS, yb_dev)
        hb[r, y1] = hb[r, y1] + ym[r]
        send(hb.at[r, y1], ya.at[r], base + Y_RS + 2, ya_dev)
        arrive(yz.at[r], base + Y_RS + 1, yb_dev)
        arrive(ya.at[r], base + Y_RS + 2, ya_dev)
        zs[r] = hb[r, y] + yz[r] + ya[r]
        for k in range(1, 8):
            dev, other_hi, other_lo = z_dev(k)
            send(
                zs.at[r, other_hi, pl.ds(pl.multiple_of(other_lo * 16, 16), 16)],
                zb.at[r, k - 1],
                base + Z_RS + k - 1,
                dev,
            )

    def scatter_users_end(r, own):
        base = r * PER_ROUND + U_RS + 3 * own
        place = slot if own else 1 - slot
        arrive(uz.at[r, own], base + 1, xb_dev)
        arrive(ua.at[r, own], base + 2, xa_dev)
        return pu[r, place, b] + uz[r, own] + ua[r, own]

    def scatter_users_far(r):
        pu[r, 1 - slot, b] = scatter_users_end(r, 0)
        send(pu.at[r, 1 - slot, b], uq.at[r], r * PER_ROUND + U_RS + 6, far_dev)

    def scatter_users_total(r):
        total = scatter_users_end(r, 1)
        if r:
            arrive(uq.at[r], r * PER_ROUND + U_RS + 6, far_dev)
            total = total + uq[r]
        return total

    def scatter_items_end(r):
        base = r * PER_ROUND
        total = zs[r, zhi, pl.ds(pl.multiple_of(c * 16, 16), 16)]
        for k in range(1, 8):
            arrive(zb.at[r, k - 1], base + Z_RS + k - 1, z_dev(8 - k)[0])
            total = total + zb[r, k - 1]
        return total

    def store_items(r, m, value):
        first = 2 * m % 4
        pi[r, m // 2, first : first + 2] = value.reshape(2, 2, 64, 256)

    def scatter(r):
        if r:
            scatter_users_forward(r, 0)
        scatter_items_y(r)
        scatter_users_forward(r, 1)
        if r:
            scatter_users_far(r)
        scatter_items_z(r)
        users = scatter_users_total(r)
        items = scatter_items_end(r)
        return users, items

    def place_tiles(h):
        own_tiles[h].wait()
        arrive(tbuf[h].at[1, pl.ds(0, GROUP)], TILES + h, pair_dev)

        def place(row, carry):
            at_row = pl.ds(pl.multiple_of(h * 512 + row * 128, 128), 128)
            for col in range(8):
                at_col = slice(col * 128, (col + 1) * 128)
                spot = (2 * h + c % 2) * PLACES + row * 8 + col
                tile = tbuf[h][0, sints[c, 4, spot]] + tbuf[h][1, sints[pair, 4, spot]]
                ah[at_row, at_col], al[at_row, at_col] = split2(tile)
                ath[at_col, at_row], atl[at_col, at_row] = split2(tile.T)
            return carry

        lax.fori_loop(0, 4, place, 0)

    to_scalars = pltpu.make_async_copy(gints, sints, lsem.at[2])

    def loss_gradient():
        gather_start(0, uf_ref[...], if_ref[...])
        for k in range(1, 4):
            dev, other = hot_dev(k)
            send(gints.at[c], gints.at[c], INTS + k - 1, dev)
        for h in range(2):
            send(
                tiles_ref.at[pl.ds((2 * h + 1 - c % 2) * GROUP, GROUP)],
                tbuf[h].at[1, pl.ds(0, GROUP)],
                TILES + h,
                pair_dev,
            )
        gather_users_forward(0, 1)
        gather_items_z(0)
        for k in range(1, 4):
            dev, other = hot_dev(4 - k)
            arrive(gints.at[other], INTS + k - 1, dev)
        to_scalars.start()
        for h in range(4):
            span = slice(h * 256, (h + 1) * 256)
            buyers = jnp.where(gints[h, 1:2, :] == c, gints[h, 0:1, :], -1)
            rows = lax.broadcasted_iota(jnp.int32, (512, 256), 0)
            ohu[:, span] = jnp.where(rows == buyers, 1.0, 0.0).astype(BF16)
            rows = lax.broadcasted_iota(jnp.int32, (1024, 256), 0)
            chosen = jnp.where(rows == gints[h, 2:3, :], 1.0, 0.0)
            others = jnp.where(rows == gints[h, 3:4, :], 1.0, 0.0)
            ohd[:, span] = (chosen - others).astype(BF16)
        gather_items_y(0)
        gather_users_end(0, 1)
        ut[0], ut[1], ut[2] = split3(ub[0, slot].reshape(512, 256).T)
        gather_items_end(0)
        dt[0], dt[1], dt[2] = split3(ib[0].reshape(1024, 256).T)
        for h in range(4):
            span = slice(h * 256, (h + 1) * 256)
            hot, signed = ohu[:, span], ohd[:, span]
            buyer = dot(ut[0], hot) + dot(ut[1], hot) + dot(ut[2], hot)
            differ = dot(dt[0], signed) + dot(dt[1], signed) + dot(dt[2], signed)
            margin = jnp.sum(buyer * differ, axis=0, keepdims=True)
            small = jnp.exp(-jnp.abs(margin))
            coef = -jnp.where(margin >= 0, small, 1.0) / (1.0 + small)
            wu[0, :, span], wu[1, :, span] = split2(coef * buyer)
            wd[0, :, span], wd[1, :, span] = split2(coef * differ)
        for m in range(4):
            left = ohd[m * 256 : (m + 1) * 256, :]
            store_items(0, m, dot_nt(left, wu[0]) + dot_nt(left, wu[1]))
        scatter_items_core(0)
        sums = dot_nt(ohu[...], wd[0]) + dot_nt(ohu[...], wd[1])
        pu[0, slot] = sums.reshape(4, 128, 256)
        scatter_users_start(0, 1)
        return scatter(0)

    def layer(r, users, items):
        gather_start(r, users, items)
        if r == 1:
            to_scalars.wait()
            place_tiles(0)
        gather_users_far(r)
        gather_users_forward(r, 1)
        gather_items_z(r)
        if r == 1:
            place_tiles(1)
        gather_users_forward(r, 0)
        gather_items_y(r)
        gather_users_end(r, 1)
        gather_users_end(r, 0)
        uh, ul = split2(ub[r].reshape(1024, 256))
        for m in range(4):
            rows = slice(m * 256, (m + 1) * 256)
            store_items(r, m, dot(ath[rows], uh) + dot(ath[rows], ul) + dot(atl[rows], uh))
        scatter_items_core(r)
        gather_items_end(r)
        xh, xl = split2(ib[r].reshape(1024, 256))
        for own in range(2):
            place = slot if own else 1 - slot
            rows = pl.ds(pl.multiple_of(place * 512, 512), 512)
            sums = dot(ah[rows], xh) + dot(ah[rows], xl) + dot(al[rows], xh)
            pu[r, place] = sums.reshape(4, 128, 256)
            scatter_users_start(r, own)
        users, items = scatter(r)
        return gu[...] + users, gi[...] + items

    def rounds():
        users, items = loss_gradient()
        gu[...] = users
        gi[...] = items
        for r in range(1, ROUNDS):
            users, items = layer(r, users, items)
        return users, items

    users, items = rounds()
    uo_ref[...] = users / (LAYERS + 1.0)
    io_ref[...] = items / (LAYERS + 1.0)
    for copy in started:
        copy.wait_send()


def body(user_final, item_final, tiles, tile_rows, tile_cols, tile_count, triplets):
    slots = tiles.shape[0]
    buyers = triplets[:, 0] % 2048
    chosen = triplets[:, 1] // 256 * 64 + triplets[:, 1] % 64
    others = triplets[:, 2] // 256 * 64 + triplets[:, 2] % 64
    slot = jnp.arange(slots, dtype=jnp.int32)
    spot = slot // GROUP * PLACES + tile_rows // 4 * 8 + tile_cols
    spot = jnp.where(slot < tile_count[0], spot, -1)
    match = spot[None, :] == jnp.arange(4 * PLACES, dtype=jnp.int32)[:, None]
    source = GROUP + jnp.sum(jnp.where(match, slot % GROUP - GROUP, 0), axis=1)
    source = jnp.concatenate([source, source])
    blank = jnp.zeros_like(source)
    ints = jnp.stack(
        [
            buyers // 512 * 128 + buyers % 128,
            buyers // 128 % 4,
            chosen,
            others,
            source,
            blank,
            blank,
            blank,
        ]
    ).astype(jnp.int32)
    vmem = pl.BlockSpec(memory_space=pltpu.VMEM)
    return pl.pallas_call(
        kernel,
        out_shape=(
            jax.ShapeDtypeStruct((128, 256), F32),
            jax.ShapeDtypeStruct((16, 256), F32),
        ),
        in_specs=[vmem, vmem, vmem, pl.BlockSpec(memory_space=pl.ANY)],
        out_specs=(vmem, vmem),
        scratch_shapes=[
            pltpu.VMEM((4, 8, 256), jnp.int32),
            pltpu.SMEM((4, 8, 256), jnp.int32),
            pltpu.VMEM((2, GROUP + 1, 128, 128), F32),
            pltpu.VMEM((2, GROUP + 1, 128, 128), F32),
            pltpu.VMEM((1024, 1024), BF16),
            pltpu.VMEM((1024, 1024), BF16),
            pltpu.VMEM((1024, 1024), BF16),
            pltpu.VMEM((1024, 1024), BF16),
            pltpu.VMEM((512, 1024), BF16),
            pltpu.VMEM((1024, 1024), BF16),
            pltpu.VMEM((3, 256, 512), BF16),
            pltpu.VMEM((3, 256, 1024), BF16),
            pltpu.VMEM((2, 256, 1024), BF16),
            pltpu.VMEM((2, 256, 1024), BF16),
            pltpu.VMEM((ROUNDS, 2, 4, 128, 256), F32),
            pltpu.VMEM((ROUNDS, 2, 4, 2, 64, 256), F32),
            pltpu.VMEM((ROUNDS, 2, 4, 128, 256), F32),
            pltpu.VMEM((ROUNDS, 2, 4, 2, 64, 256), F32),
            pltpu.VMEM((ROUNDS, 2, 128, 256), F32),
            pltpu.VMEM((ROUNDS, 2, 128, 256), F32),
            pltpu.VMEM((ROUNDS, 2, 128, 256), F32),
            pltpu.VMEM((ROUNDS, 128, 256), F32),
            pltpu.VMEM((ROUNDS, 2, 4, 64, 256), F32),
            pltpu.VMEM((ROUNDS, 4, 2, 64, 256), F32),
            pltpu.VMEM((ROUNDS, 2, 64, 256), F32),
            pltpu.VMEM((ROUNDS, 2, 64, 256), F32),
            pltpu.VMEM((ROUNDS, 2, 64, 256), F32),
            pltpu.VMEM((ROUNDS, 2, 64, 256), F32),
            pltpu.VMEM((ROUNDS, 7, 16, 256), F32),
            pltpu.VMEM((128, 256), F32),
            pltpu.VMEM((16, 256), F32),
            pltpu.SemaphoreType.DMA((COPIES,)),
            pltpu.SemaphoreType.DMA((COPIES,)),
            pltpu.SemaphoreType.DMA((3,)),
        ],
        compiler_params=pltpu.CompilerParams(
            collective_id=0, has_side_effects=True, vmem_limit_bytes=52 * 1024 * 1024
        ),
        name="propagate",
    )(ints, user_final, item_final, tiles)


def solution(mesh):
    placed = (
        P(("user", "item", "hot"), None),
        P(("user", "item", "hot"), None),
        P(("user", "item", "hot"), None, None),
        P(("user", "item", "hot")),
        P(("user", "item", "hot")),
        P(("user", "item", "hot")),
        P(("user", "item", "hot"), None),
    )
    return jax.shard_map(
        body,
        mesh=mesh,
        in_specs=placed,
        out_specs=(P(("user", "item", "hot"), None), P(("user", "item", "hot"), None)),
        check_vma=False,
    )
```

```python
import jax
import jax.numpy as jnp
from jax import lax
from jax.experimental import pallas as pl
from jax.experimental.pallas import tpu as pltpu
from jax.sharding import PartitionSpec as P

MESH = pl.DeviceIdType.MESH
F32 = jnp.float32
BF16 = jnp.bfloat16
LAYERS = 2


ROUNDS = LAYERS + 1
GROUP = 12
PLACES = 32

CHUNKS = 4
CHUNK = 32
PIECES = 6
PIECE = 4
EARLY = 4

U_AG = 0
Z_AG = U_AG + 7 * CHUNKS
Y_AG = Z_AG + 7
C_AG = Y_AG + 24
C_RS = C_AG + 11
Y_RS = C_RS + 4
Z_RS = Y_RS + 24
U_RS = Z_RS + 7
PER_ROUND = U_RS + 7 * CHUNKS
INTS = PER_ROUND * ROUNDS
TILES = INTS + 3
COPIES = TILES + PIECES
NEAR_FIRST = (1, 7, 2, 6, 3, 5, 4)
FAR_FIRST = (4, 5, 3, 6, 2, 7, 1)


def split2(x):
    hi = x.astype(BF16)
    return hi, (x - hi.astype(F32)).astype(BF16)


def split3(x):
    hi = x.astype(BF16)
    rest = x - hi.astype(F32)
    mid = rest.astype(BF16)
    return hi, mid, (rest - mid.astype(F32)).astype(BF16)


def dot(a, b):
    return jnp.dot(a, b, preferred_element_type=F32)


def dot_nt(a, b):
    return lax.dot_general(a, b, (((1,), (1,)), ((), ())), preferred_element_type=F32)


def kernel(
    ints_ref,
    uf_ref,
    if_ref,
    tiles_ref,
    uo_ref,
    io_ref,
    gints,
    sints,
    tbuf0,
    tbuf1,
    ah,
    al,
    ath,
    atl,
    ohu,
    ohd,
    buy,
    ut,
    dt,
    wd,
    wu,
    ub,
    ib,
    pu,
    pi,
    um,
    ua,
    uz,
    uq,
    rc,
    hb,
    ym,
    ya,
    yz,
    zs,
    zb,
    gu,
    gi,
    ssem,
    rsem,
    lsem,
):
    a = lax.axis_index("user")
    b = lax.axis_index("item")
    c = lax.axis_index("hot")
    core = a % 2
    y = (a // 2) % 4
    zhi = a // 8
    z = zhi * 4 + c

    def user_index(zhi_, y_, core_):
        return (zhi_ * 4 + y_) * 2 + core_

    def ring(v):
        even = v + 1 - 2 * (v % 2)
        odd = 3 - v
        first = (1 - core) * even + core * odd
        second = (1 - core) * odd + core * even
        return first, second, (v + 2) % 4

    x1, x2, xo = ring(b)
    y1, y2, yo = ring(y)
    ya_dev = (user_index(zhi, y1, core), b, c)
    yb_dev = (user_index(zhi, y2, core), b, c)
    xa_dev = (a, x1, c)
    xb_dev = (a, x2, c)
    tbuf = (tbuf0, tbuf1)
    slot = c // 2
    pair = c + 1 - 2 * (c % 2)
    pair_dev = (a, b, pair)
    far_dev = (a, b, (c + 2) % 4)
    sib = (user_index(zhi, y, 1 - core), b, c)

    def z_dev(k):
        other = (z + k) % 8
        return (user_index(other // 4, y, core), b, other % 4), other // 4, other % 4

    def hot_dev(k):
        other = (c + k) % 4
        return (a, b, other), other

    started = []

    def send(src, dst, index, dev):
        copy = pltpu.make_async_remote_copy(
            src_ref=src,
            dst_ref=dst,
            send_sem=ssem.at[index],
            recv_sem=rsem.at[index],
            device_id=dev,
            device_id_type=MESH,
        )
        copy.start()
        started.append(copy)

    def arrive(dst, index, dev):
        pltpu.make_async_remote_copy(
            src_ref=dst,
            dst_ref=dst,
            send_sem=ssem.at[index],
            recv_sem=rsem.at[index],
            device_id=dev,
            device_id_type=MESH,
        ).wait_recv()

    barrier = pltpu.get_barrier_semaphore()
    peers = [xa_dev, xb_dev, ya_dev, yb_dev, sib] + [z_dev(k)[0] for k in range(1, 8)]
    for dev in peers:
        pl.semaphore_signal(barrier, inc=1, device_id=dev, device_id_type=MESH)
    own_tiles = [
        pltpu.make_async_copy(
            tiles_ref.at[pl.ds((2 * h + c % 2) * GROUP, GROUP)],
            tbuf[h].at[0, pl.ds(0, GROUP)],
            lsem.at[h],
        )
        for h in range(2)
    ]
    for copy in own_tiles:
        copy.start()
    for h in range(2):
        tbuf[h][0, GROUP] = jnp.zeros((128, 128), F32)
        tbuf[h][1, GROUP] = jnp.zeros((128, 128), F32)
    gints[c] = ints_ref[...]
    pl.semaphore_wait(barrier, len(peers))

    def chunk(q):
        return pl.ds(q * CHUNK, CHUNK)

    def place_of(own):
        return slot if own else 1 - slot

    def along_z(k):
        other = (z + k) % 8
        return other // 4, other % 4

    def gather_users_start(r, users):
        base = r * PER_ROUND + U_AG
        ub[r, slot, b] = users
        for q in range(CHUNKS):
            mine = ub.at[r, slot, b, chunk(q)]
            if r:
                send(mine, mine, base + 6 * CHUNKS + q, far_dev)
            send(mine, mine, base + q, xa_dev)
            send(mine, mine, base + CHUNKS + q, xb_dev)

    def gather_users_far(r):
        base = r * PER_ROUND + U_AG
        for q in range(CHUNKS):
            other = ub.at[r, 1 - slot, b, chunk(q)]
            arrive(other, base + 6 * CHUNKS + q, far_dev)
            send(other, other, base + 3 * CHUNKS + q, xa_dev)
            send(other, other, base + 4 * CHUNKS + q, xb_dev)

    def gather_users_forward(r, own):
        base = r * PER_ROUND + U_AG + (0 if own else 3 * CHUNKS)
        for q in range(CHUNKS):
            block = ub.at[r, place_of(own), x1, chunk(q)]
            arrive(block, base + q, xa_dev)
            send(block, block, base + 2 * CHUNKS + q, xb_dev)

    def gather_users_end(r, own):
        base = r * PER_ROUND + U_AG + (0 if own else 3 * CHUNKS)
        for q in range(CHUNKS):
            arrive(ub.at[r, place_of(own), x2, chunk(q)], base + CHUNKS + q, xb_dev)
        for q in range(CHUNKS):
            arrive(ub.at[r, place_of(own), xo, chunk(q)], base + 2 * CHUNKS + q, xb_dev)

    def scatter_users_start(r, own):
        base = r * PER_ROUND + U_RS + 3 * CHUNKS * own
        place = place_of(own)
        for q in range(CHUNKS):
            send(pu.at[r, place, xo, chunk(q)], um.at[r, own, chunk(q)], base + q, xb_dev)
        for q in range(CHUNKS):
            send(pu.at[r, place, x2, chunk(q)], uz.at[r, own, chunk(q)], base + CHUNKS + q, xb_dev)

    def scatter_users_forward(r, own):
        base = r * PER_ROUND + U_RS + 3 * CHUNKS * own
        place = place_of(own)
        for q in range(CHUNKS):
            arrive(um.at[r, own, chunk(q)], base + q, xb_dev)
            pu[r, place, x1, chunk(q)] = pu[r, place, x1, chunk(q)] + um[r, own, chunk(q)]
            sums = pu.at[r, place, x1, chunk(q)]
            send(sums, ua.at[r, own, chunk(q)], base + 2 * CHUNKS + q, xa_dev)

    def scatter_users_sum(r, own):
        base = r * PER_ROUND + U_RS + 3 * CHUNKS * own
        place = place_of(own)
        for q in range(CHUNKS):
            arrive(uz.at[r, own, chunk(q)], base + CHUNKS + q, xb_dev)
            arrive(ua.at[r, own, chunk(q)], base + 2 * CHUNKS + q, xa_dev)
            sums = pu[r, place, b, chunk(q)] + uz[r, own, chunk(q)] + ua[r, own, chunk(q)]
            pu[r, place, b, chunk(q)] = sums
            if not own:
                index = r * PER_ROUND + U_RS + 6 * CHUNKS + q
                send(pu.at[r, place, b, chunk(q)], uq.at[r, chunk(q)], index, far_dev)

    def scatter_users_total(r):
        scatter_users_sum(r, 1)
        total = pu[r, slot, b]
        if r:
            for q in range(CHUNKS):
                arrive(uq.at[r, chunk(q)], r * PER_ROUND + U_RS + 6 * CHUNKS + q, far_dev)
            total = total + uq[r]
        return total

    def gather_items_start(r, items):
        base = r * PER_ROUND
        ib[r, zhi, y, core, c] = items
        mine = ib.at[r, zhi, y, core, c]
        for k in FAR_FIRST:
            send(mine, mine, base + Z_AG + k - 1, z_dev(k)[0])
        send(mine, mine, base + Y_AG, ya_dev)
        send(mine, mine, base + Y_AG + 8, yb_dev)

    def gather_items_z(r, steps):
        base = r * PER_ROUND
        for k in steps:
            hi, lo = along_z(k)
            piece = ib.at[r, hi, y, core, lo]
            arrive(piece, base + Z_AG + (8 - k) - 1, z_dev(k)[0])
            send(piece, piece, base + Y_AG + k, ya_dev)
            send(piece, piece, base + Y_AG + 8 + k, yb_dev)

    def gather_items_forward(r, steps):
        base = r * PER_ROUND
        for k in steps:
            hi, lo = along_z(k)
            piece = ib.at[r, hi, y1, core, lo]
            arrive(piece, base + Y_AG + k, ya_dev)
            send(piece, piece, base + Y_AG + 16 + k, yb_dev)

    def gather_items_core(r):
        base = r * PER_ROUND
        for index, other in ((0, y), (1 + core, y1)):
            block = ib.at[r, :, other, core]
            send(block, block, base + C_AG + index, sib)
        for k in (0,) + NEAR_FIRST:
            hi, lo = along_z(k)
            arrive(ib.at[r, hi, y2, core, lo], base + Y_AG + 8 + k, yb_dev)
        block = ib.at[r, :, y2, core]
        send(block, block, base + C_AG + 2 - core, sib)
        for k in (0,) + NEAR_FIRST:
            hi, lo = along_z(k)
            piece = ib.at[r, hi, yo, core, lo]
            arrive(piece, base + Y_AG + 16 + k, yb_dev)
            send(piece, piece, base + C_AG + 3 + k, sib)

    def gather_items_end(r):
        base = r * PER_ROUND
        for index, other in ((0, y), (1, y + 1 - 2 * (y % 2)), (2, 3 - y)):
            arrive(ib.at[r, :, other, 1 - core], base + C_AG + index, sib)
        for k in (0,) + NEAR_FIRST:
            hi, lo = along_z(k)
            arrive(ib.at[r, hi, yo, 1 - core, lo], base + C_AG + 3 + k, sib)

    def scatter_items_core(r):
        base = r * PER_ROUND
        for k, other in ((2, yo), (1, y + 1 - 2 * (y % 2)), (3, 3 - y), (0, y)):
            send(pi.at[r, :, other, 1 - core], rc.at[r, :, other], base + C_RS + k, sib)

    def scatter_items_y(r):
        base = r * PER_ROUND

        def halves(k, other):
            arrive(rc.at[r, :, other], base + C_RS + k, sib)
            sums = pi[r, :, other, core] + rc[r, :, other]
            hb[r, other] = sums.reshape(8, 16, 256)

        halves(2, yo)
        for k in FAR_FIRST + (0,):
            at = (z + k) % 8
            send(hb.at[r, yo, at], ym.at[r, at], base + Y_RS + k, yb_dev)
        halves(1, y + 1 - 2 * (y % 2))
        halves(3, 3 - y)
        for k in FAR_FIRST + (0,):
            at = (z + k) % 8
            send(hb.at[r, y2, at], yz.at[r, at], base + Y_RS + 8 + k, yb_dev)
        halves(0, y)

    def scatter_items_forward(r):
        base = r * PER_ROUND
        for k in FAR_FIRST + (0,):
            at = (z + k) % 8
            arrive(ym.at[r, at], base + Y_RS + k, yb_dev)
            hb[r, y1, at] = hb[r, y1, at] + ym[r, at]
            send(hb.at[r, y1, at], ya.at[r, at], base + Y_RS + 16 + k, ya_dev)

    def scatter_items_z(r):
        base = r * PER_ROUND
        for k in FAR_FIRST + (0,):
            at = (z + k) % 8
            arrive(yz.at[r, at], base + Y_RS + 8 + k, yb_dev)
            arrive(ya.at[r, at], base + Y_RS + 16 + k, ya_dev)
            zs[r, at] = hb[r, y, at] + yz[r, at] + ya[r, at]
            if k:
                send(zs.at[r, at], zb.at[r, k - 1], base + Z_RS + k - 1, z_dev(k)[0])

    def scatter_items_total(r):
        base = r * PER_ROUND
        total = zs[r, z]
        for k in NEAR_FIRST:
            arrive(zb.at[r, k - 1], base + Z_RS + k - 1, z_dev(8 - k)[0])
            total = total + zb[r, k - 1]
        return total

    def store_items(r, m, value):
        first = 2 * m % 4
        pi[r, m // 2, first : first + 2] = value.reshape(2, 2, 64, 256)

    def scatter(r):
        if r:
            scatter_users_forward(r, 0)
        scatter_items_y(r)
        scatter_users_forward(r, 1)
        if r:
            scatter_users_sum(r, 0)
        scatter_items_forward(r)
        scatter_items_z(r)
        users = scatter_users_total(r)
        if r:
            users = gu[...] + users
        else:
            gu[...] = users
        if r < LAYERS:
            gather_users_start(r + 1, users)
        items = scatter_items_total(r)
        if r:
            items = gi[...] + items
        else:
            gi[...] = items
        return users, items

    def send_tiles(first, last):
        for n in range(first, last):
            h = n // 3
            start = (2 * h + 1 - c % 2) * GROUP + n % 3 * PIECE
            send(
                tiles_ref.at[pl.ds(start, PIECE)],
                tbuf[h].at[1, pl.ds(n % 3 * PIECE, PIECE)],
                TILES + n,
                pair_dev,
            )

    def place_tiles(h):
        own_tiles[h].wait()
        for n in range(3 * h, 3 * h + 3):
            arrive(tbuf[h].at[1, pl.ds(n % 3 * PIECE, PIECE)], TILES + n, pair_dev)

        def place(row, carry):
            at_row = pl.ds(pl.multiple_of(h * 512 + row * 128, 128), 128)
            for col in range(8):
                at_col = slice(col * 128, (col + 1) * 128)
                spot = (2 * h + c % 2) * PLACES + row * 8 + col
                tile = tbuf[h][0, sints[c, 4, spot]] + tbuf[h][1, sints[pair, 4, spot]]
                ah[at_row, at_col], al[at_row, at_col] = split2(tile)
                ath[at_col, at_row], atl[at_col, at_row] = split2(tile.T)
            return carry

        lax.fori_loop(0, 4, place, 0)

    to_scalars = pltpu.make_async_copy(gints, sints, lsem.at[2])

    def loss_gradient():
        for k in range(1, 4):
            dev, other = hot_dev(k)
            send(gints.at[c], gints.at[c], INTS + k - 1, dev)
        gather_items_start(0, if_ref[...])
        gather_users_start(0, uf_ref[...])
        send_tiles(0, EARLY)
        gather_items_z(0, NEAR_FIRST[:2])
        gather_users_forward(0, 1)
        gather_items_forward(0, (0,))
        gather_items_z(0, NEAR_FIRST[2:])
        gather_items_forward(0, NEAR_FIRST[:2])
        for k in range(1, 4):
            dev, other = hot_dev(4 - k)
            arrive(gints.at[other], INTS + k - 1, dev)
        to_scalars.start()
        for h in range(4):
            span = slice(h * 256, (h + 1) * 256)
            buyers = jnp.where(gints[h, 1:2, :] == c, gints[h, 0:1, :], -1)
            rows = lax.broadcasted_iota(jnp.int32, (512, 256), 0)
            ohu[:, span] = jnp.where(rows == buyers, 1.0, 0.0).astype(BF16)
        gather_items_forward(0, NEAR_FIRST[2:])
        for h in range(4):
            span = slice(h * 256, (h + 1) * 256)
            rows = lax.broadcasted_iota(jnp.int32, (1024, 256), 0)
            chosen = jnp.where(rows == gints[h, 2:3, :], 1.0, 0.0)
            others = jnp.where(rows == gints[h, 3:4, :], 1.0, 0.0)
            ohd[:, span] = (chosen - others).astype(BF16)
        gather_items_core(0)
        gather_users_end(0, 1)
        ut[0], ut[1], ut[2] = split3(ub[0, slot].reshape(512, 256).T)
        for h in range(4):
            span = slice(h * 256, (h + 1) * 256)
            hot = ohu[:, span]
            buy[:, span] = dot(ut[0], hot) + dot(ut[1], hot) + dot(ut[2], hot)
        gather_items_end(0)
        dt[0], dt[1], dt[2] = split3(ib[0].reshape(1024, 256).T)
        for h in range(4):
            span = slice(h * 256, (h + 1) * 256)
            buyer, signed = buy[:, span], ohd[:, span]
            differ = dot(dt[0], signed) + dot(dt[1], signed) + dot(dt[2], signed)
            margin = jnp.sum(buyer * differ, axis=0, keepdims=True)
            small = jnp.exp(-jnp.abs(margin))
            coef = -jnp.where(margin >= 0, small, 1.0) / (1.0 + small)
            wu[0, :, span], wu[1, :, span] = split2(coef * buyer)
            wd[0, :, span], wd[1, :, span] = split2(coef * differ)
        for m in range(4):
            left = ohd[m * 256 : (m + 1) * 256, :]
            store_items(0, m, dot_nt(left, wu[0]) + dot_nt(left, wu[1]))
        scatter_items_core(0)
        sums = dot_nt(ohu[...], wd[0]) + dot_nt(ohu[...], wd[1])
        pu[0, slot] = sums.reshape(4, 128, 256)
        scatter_users_start(0, 1)
        return scatter(0)

    def layer(r, items):
        gather_items_start(r, items)
        if r == 1:
            send_tiles(EARLY, PIECES)
            to_scalars.wait()
            place_tiles(0)
        gather_items_z(r, NEAR_FIRST[:2])
        gather_users_forward(r, 1)
        gather_items_forward(r, (0,))
        gather_items_z(r, NEAR_FIRST[2:])
        gather_users_far(r)
        gather_items_forward(r, NEAR_FIRST)
        gather_items_core(r)
        gather_users_forward(r, 0)
        gather_items_end(r)
        if r == 1:
            place_tiles(1)
        xh, xl = split2(ib[r].reshape(1024, 256))
        for own in range(2):
            place = place_of(own)
            rows = pl.ds(pl.multiple_of(place * 512, 512), 512)
            sums = dot(ah[rows], xh) + dot(ah[rows], xl) + dot(al[rows], xh)
            pu[r, place] = sums.reshape(4, 128, 256)
            scatter_users_start(r, own)
        gather_users_end(r, 1)
        gather_users_end(r, 0)
        uh, ul = split2(ub[r].reshape(1024, 256))
        for m in range(4):
            rows = slice(m * 256, (m + 1) * 256)
            store_items(r, m, dot(ath[rows], uh) + dot(ath[rows], ul) + dot(atl[rows], uh))
        scatter_items_core(r)
        return scatter(r)

    def rounds():
        users, items = loss_gradient()
        for r in range(1, ROUNDS):
            users, items = layer(r, items)
        return users, items

    users, items = rounds()
    uo_ref[...] = users / (LAYERS + 1.0)
    io_ref[...] = items / (LAYERS + 1.0)
    for copy in started:
        copy.wait_send()


def body(user_final, item_final, tiles, tile_rows, tile_cols, tile_count, triplets):
    slots = tiles.shape[0]
    buyers = triplets[:, 0] % 2048
    chosen = triplets[:, 1] // 256 * 64 + triplets[:, 1] % 64
    others = triplets[:, 2] // 256 * 64 + triplets[:, 2] % 64
    slot = jnp.arange(slots, dtype=jnp.int32)
    spot = slot // GROUP * PLACES + tile_rows // 4 * 8 + tile_cols
    spot = jnp.where(slot < tile_count[0], spot, -1)
    match = spot[None, :] == jnp.arange(4 * PLACES, dtype=jnp.int32)[:, None]
    source = GROUP + jnp.sum(jnp.where(match, slot % GROUP - GROUP, 0), axis=1)
    source = jnp.concatenate([source, source])
    blank = jnp.zeros_like(source)
    ints = jnp.stack(
        [
            buyers // 512 * 128 + buyers % 128,
            buyers // 128 % 4,
            chosen,
            others,
            source,
            blank,
            blank,
            blank,
        ]
    ).astype(jnp.int32)
    vmem = pl.BlockSpec(memory_space=pltpu.VMEM)
    return pl.pallas_call(
        kernel,
        out_shape=(
            jax.ShapeDtypeStruct((128, 256), F32),
            jax.ShapeDtypeStruct((16, 256), F32),
        ),
        in_specs=[vmem, vmem, vmem, pl.BlockSpec(memory_space=pl.ANY)],
        out_specs=(vmem, vmem),
        scratch_shapes=[
            pltpu.VMEM((4, 8, 256), jnp.int32),
            pltpu.SMEM((4, 8, 256), jnp.int32),
            pltpu.VMEM((2, GROUP + 1, 128, 128), F32),
            pltpu.VMEM((2, GROUP + 1, 128, 128), F32),
            pltpu.VMEM((1024, 1024), BF16),
            pltpu.VMEM((1024, 1024), BF16),
            pltpu.VMEM((1024, 1024), BF16),
            pltpu.VMEM((1024, 1024), BF16),
            pltpu.VMEM((512, 1024), BF16),
            pltpu.VMEM((1024, 1024), BF16),
            pltpu.VMEM((256, 1024), F32),
            pltpu.VMEM((3, 256, 512), BF16),
            pltpu.VMEM((3, 256, 1024), BF16),
            pltpu.VMEM((2, 256, 1024), BF16),
            pltpu.VMEM((2, 256, 1024), BF16),
            pltpu.VMEM((ROUNDS, 2, 4, 128, 256), F32),
            pltpu.VMEM((ROUNDS, 2, 4, 2, 4, 16, 256), F32),
            pltpu.VMEM((ROUNDS, 2, 4, 128, 256), F32),
            pltpu.VMEM((ROUNDS, 2, 4, 2, 64, 256), F32),
            pltpu.VMEM((ROUNDS, 2, 128, 256), F32),
            pltpu.VMEM((ROUNDS, 2, 128, 256), F32),
            pltpu.VMEM((ROUNDS, 2, 128, 256), F32),
            pltpu.VMEM((ROUNDS, 128, 256), F32),
            pltpu.VMEM((ROUNDS, 2, 4, 64, 256), F32),
            pltpu.VMEM((ROUNDS, 4, 8, 16, 256), F32),
            pltpu.VMEM((ROUNDS, 8, 16, 256), F32),
            pltpu.VMEM((ROUNDS, 8, 16, 256), F32),
            pltpu.VMEM((ROUNDS, 8, 16, 256), F32),
            pltpu.VMEM((ROUNDS, 8, 16, 256), F32),
            pltpu.VMEM((ROUNDS, 7, 16, 256), F32),
            pltpu.VMEM((128, 256), F32),
            pltpu.VMEM((16, 256), F32),
            pltpu.SemaphoreType.DMA((COPIES,)),
            pltpu.SemaphoreType.DMA((COPIES,)),
            pltpu.SemaphoreType.DMA((3,)),
        ],
        compiler_params=pltpu.CompilerParams(
            collective_id=0, has_side_effects=True, vmem_limit_bytes=52 * 1024 * 1024
        ),
        name="propagate",
    )(ints, user_final, item_final, tiles)


def solution(mesh):
    placed = (
        P(("user", "item", "hot"), None),
        P(("user", "item", "hot"), None),
        P(("user", "item", "hot"), None, None),
        P(("user", "item", "hot")),
        P(("user", "item", "hot")),
        P(("user", "item", "hot")),
        P(("user", "item", "hot"), None),
    )
    return jax.shard_map(
        body,
        mesh=mesh,
        in_specs=placed,
        out_specs=(P(("user", "item", "hot"), None), P(("user", "item", "hot"), None)),
        check_vma=False,
    )
```

```python
import jax
import jax.numpy as jnp
from jax import lax
from jax.experimental import pallas as pl
from jax.experimental.pallas import tpu as pltpu
from jax.sharding import PartitionSpec as P

MESH = pl.DeviceIdType.MESH
F32 = jnp.float32
BF16 = jnp.bfloat16
LAYERS = 2


ROUNDS = LAYERS + 1
GROUP = 12
PLACES = 32

CHUNKS = 4
CHUNK = 32
PIECES = 6
PIECE = 4
EARLY = 4

U_AG = 0
Z_AG = U_AG + 7 * CHUNKS
Y_AG = Z_AG + 7
C_AG = Y_AG + 24
C_RS = C_AG + 32
Y_RS = C_RS + 4
Z_RS = Y_RS + 24
U_RS = Z_RS + 7
PER_ROUND = U_RS + 7 * CHUNKS
INTS = PER_ROUND * ROUNDS
TILES = INTS + 3
COPIES = TILES + PIECES
NEAR_FIRST = (1, 7, 2, 6, 3, 5, 4)
FAR_FIRST = (4, 5, 3, 6, 2, 7, 1)


def split2(x):
    hi = x.astype(BF16)
    return hi, (x - hi.astype(F32)).astype(BF16)


def split3(x):
    hi = x.astype(BF16)
    rest = x - hi.astype(F32)
    mid = rest.astype(BF16)
    return hi, mid, (rest - mid.astype(F32)).astype(BF16)


def dot(a, b):
    return jnp.dot(a, b, preferred_element_type=F32)


def dot_nt(a, b):
    return lax.dot_general(a, b, (((1,), (1,)), ((), ())), preferred_element_type=F32)


def kernel(
    ints_ref,
    uf_ref,
    if_ref,
    tiles_ref,
    uo_ref,
    io_ref,
    gints,
    sints,
    tbuf0,
    tbuf1,
    ah,
    al,
    ath,
    atl,
    ohu,
    ohd,
    buy,
    ut,
    dt,
    wd,
    wu,
    ub,
    ib,
    pu,
    pi,
    um,
    ua,
    uz,
    uq,
    rc,
    hb,
    ym,
    ya,
    yz,
    zs,
    zb,
    gu,
    gi,
    ssem,
    rsem,
    lsem,
):
    a = lax.axis_index("user")
    b = lax.axis_index("item")
    c = lax.axis_index("hot")
    core = a % 2
    y = (a // 2) % 4
    zhi = a // 8
    z = zhi * 4 + c

    def user_index(zhi_, y_, core_):
        return (zhi_ * 4 + y_) * 2 + core_

    def ring(v):
        even = v + 1 - 2 * (v % 2)
        odd = 3 - v
        first = (1 - core) * even + core * odd
        second = (1 - core) * odd + core * even
        return first, second, (v + 2) % 4

    x1, x2, xo = ring(b)
    xa_dev = (a, x1, c)
    xb_dev = (a, x2, c)
    xo_dev = (a, xo, c)
    tbuf = (tbuf0, tbuf1)
    yb = (ym, ya, yz)
    slot = c // 2
    pair = c + 1 - 2 * (c % 2)
    pair_dev = (a, b, pair)
    far_dev = (a, b, (c + 2) % 4)
    sib = (user_index(zhi, y, 1 - core), b, c)

    def z_dev(k):
        other = (z + k) % 8
        return (user_index(other // 4, y, core), b, other % 4), other // 4, other % 4

    def y_dev(k):
        other = (y + k) % 4
        return (user_index(zhi, other, core), b, c)

    def hot_dev(k):
        other = (c + k) % 4
        return (a, b, other), other

    started = []

    def send(src, dst, index, dev):
        copy = pltpu.make_async_remote_copy(
            src_ref=src,
            dst_ref=dst,
            send_sem=ssem.at[index],
            recv_sem=rsem.at[index],
            device_id=dev,
            device_id_type=MESH,
        )
        copy.start()
        started.append(copy)

    def arrive(dst, index, dev):
        pltpu.make_async_remote_copy(
            src_ref=dst,
            dst_ref=dst,
            send_sem=ssem.at[index],
            recv_sem=rsem.at[index],
            device_id=dev,
            device_id_type=MESH,
        ).wait_recv()

    barrier = pltpu.get_barrier_semaphore()
    peers = [xa_dev, xb_dev, xo_dev, sib]
    peers += [y_dev(k) for k in range(1, 4)] + [z_dev(k)[0] for k in range(1, 8)]
    for dev in peers:
        pl.semaphore_signal(barrier, inc=1, device_id=dev, device_id_type=MESH)
    own_tiles = [
        pltpu.make_async_copy(
            tiles_ref.at[pl.ds((2 * h + c % 2) * GROUP, GROUP)],
            tbuf[h].at[0, pl.ds(0, GROUP)],
            lsem.at[h],
        )
        for h in range(2)
    ]
    for copy in own_tiles:
        copy.start()
    for h in range(2):
        tbuf[h][0, GROUP] = jnp.zeros((128, 128), F32)
        tbuf[h][1, GROUP] = jnp.zeros((128, 128), F32)
    gints[c] = ints_ref[...]
    pl.semaphore_wait(barrier, len(peers))

    def chunk(q):
        return pl.ds(q * CHUNK, CHUNK)

    def place_of(own):
        return slot if own else 1 - slot

    def along_z(k):
        other = (z + k) % 8
        return other // 4, other % 4

    def gather_users_start(r, users):
        base = r * PER_ROUND + U_AG
        ub[r, slot, b] = users
        for q in range(CHUNKS):
            mine = ub.at[r, slot, b, chunk(q)]
            send(mine, mine, base + q, xa_dev)
            send(mine, mine, base + CHUNKS + q, xb_dev)

    def gather_users_over_z(r):
        for q in range(CHUNKS):
            mine = ub.at[r, slot, b, chunk(q)]
            send(mine, mine, r * PER_ROUND + U_AG + 6 * CHUNKS + q, far_dev)

    def gather_users_far(r, chunks):
        base = r * PER_ROUND + U_AG
        for q in chunks:
            other = ub.at[r, 1 - slot, b, chunk(q)]
            arrive(other, base + 6 * CHUNKS + q, far_dev)
            send(other, other, base + 5 * CHUNKS + q, xo_dev)
            send(other, other, base + 3 * CHUNKS + q, xa_dev)
            send(other, other, base + 4 * CHUNKS + q, xb_dev)

    def gather_users_forward(r):
        base = r * PER_ROUND + U_AG
        for q in range(CHUNKS):
            block = ub.at[r, slot, x1, chunk(q)]
            arrive(block, base + q, xa_dev)
            send(block, block, base + 2 * CHUNKS + q, xb_dev)

    def gather_users_end(r):
        base = r * PER_ROUND + U_AG
        for q in range(CHUNKS):
            arrive(ub.at[r, slot, x2, chunk(q)], base + CHUNKS + q, xb_dev)
        for q in range(CHUNKS):
            arrive(ub.at[r, slot, xo, chunk(q)], base + 2 * CHUNKS + q, xb_dev)
        if r:
            base = base + 3 * CHUNKS
            for q in range(CHUNKS):
                arrive(ub.at[r, 1 - slot, x1, chunk(q)], base + q, xa_dev)
                arrive(ub.at[r, 1 - slot, x2, chunk(q)], base + CHUNKS + q, xb_dev)
                arrive(ub.at[r, 1 - slot, xo, chunk(q)], base + 2 * CHUNKS + q, xo_dev)

    def scatter_users_start(r, own):
        base = r * PER_ROUND + U_RS + 3 * CHUNKS * own
        place = place_of(own)
        for q in range(CHUNKS):
            send(pu.at[r, place, xo, chunk(q)], um.at[r, own, chunk(q)], base + q, xb_dev)
        for q in range(CHUNKS):
            send(pu.at[r, place, x2, chunk(q)], uz.at[r, own, chunk(q)], base + CHUNKS + q, xb_dev)

    def scatter_users_forward(r, own):
        base = r * PER_ROUND + U_RS + 3 * CHUNKS * own
        place = place_of(own)
        for q in range(CHUNKS):
            arrive(um.at[r, own, chunk(q)], base + q, xb_dev)
            pu[r, place, x1, chunk(q)] = pu[r, place, x1, chunk(q)] + um[r, own, chunk(q)]
            sums = pu.at[r, place, x1, chunk(q)]
            send(sums, ua.at[r, own, chunk(q)], base + 2 * CHUNKS + q, xa_dev)

    def scatter_users_sum(r, own):
        base = r * PER_ROUND + U_RS + 3 * CHUNKS * own
        place = place_of(own)
        for q in range(CHUNKS):
            arrive(uz.at[r, own, chunk(q)], base + CHUNKS + q, xb_dev)
            arrive(ua.at[r, own, chunk(q)], base + 2 * CHUNKS + q, xa_dev)
            sums = pu[r, place, b, chunk(q)] + uz[r, own, chunk(q)] + ua[r, own, chunk(q)]
            pu[r, place, b, chunk(q)] = sums
            if not own:
                index = r * PER_ROUND + U_RS + 6 * CHUNKS + q
                send(pu.at[r, place, b, chunk(q)], uq.at[r, chunk(q)], index, far_dev)

    def scatter_users_total(r):
        scatter_users_sum(r, 1)
        total = pu[r, slot, b]
        if r:
            for q in range(CHUNKS):
                arrive(uq.at[r, chunk(q)], r * PER_ROUND + U_RS + 6 * CHUNKS + q, far_dev)
            total = total + uq[r]
        return total

    def gather_items_start(r, items):
        base = r * PER_ROUND
        ib[r, zhi, y, core, c] = items
        mine = ib.at[r, zhi, y, core, c]
        for k in FAR_FIRST:
            send(mine, mine, base + Z_AG + k - 1, z_dev(k)[0])
        pass_on(r, 0)

    def pass_on(r, k):
        base = r * PER_ROUND
        hi, lo = along_z(k)
        piece = ib.at[r, hi, y, core, lo]
        for d in (2, 1, 3):
            send(piece, piece, base + Y_AG + (d - 1) * 8 + k, y_dev(d))
        send(piece, piece, base + C_AG + k, sib)

    def gather_items_z(r, steps):
        base = r * PER_ROUND
        for k in steps:
            hi, lo = along_z(k)
            arrive(ib.at[r, hi, y, core, lo], base + Z_AG + (8 - k) - 1, z_dev(k)[0])
            pass_on(r, k)

    def gather_items_y(r, steps):
        base = r * PER_ROUND
        for k in steps:
            hi, lo = along_z(k)
            for d in (1, 3, 2):
                piece = ib.at[r, hi, (y + d) % 4, core, lo]
                arrive(piece, base + Y_AG + (3 - d) * 8 + k, y_dev(d))
                send(piece, piece, base + C_AG + d * 8 + k, sib)

    def gather_items_end(r):
        base = r * PER_ROUND
        for k in (0,) + NEAR_FIRST:
            hi, lo = along_z(k)
            for d in range(4):
                piece = ib.at[r, hi, (y + d) % 4, 1 - core, lo]
                arrive(piece, base + C_AG + d * 8 + k, sib)

    def scatter_items_core(r):
        base = r * PER_ROUND
        for d in (2, 1, 3, 0):
            other = (y + d) % 4
            send(pi.at[r, :, other, 1 - core], rc.at[r, :, other], base + C_RS + d, sib)

    def scatter_items_y(r):
        base = r * PER_ROUND
        for d in (2, 1, 3, 0):
            other = (y + d) % 4
            arrive(rc.at[r, :, other], base + C_RS + d, sib)
            sums = pi[r, :, other, core] + rc[r, :, other]
            hb[r, other] = sums.reshape(8, 16, 256)
        for k in FAR_FIRST + (0,):
            at = (z + k) % 8
            for d in (2, 1, 3):
                source = hb.at[r, (y + d) % 4, at]
                send(source, yb[d - 1].at[r, at], base + Y_RS + (d - 1) * 8 + k, y_dev(d))

    def scatter_items_z(r, steps):
        base = r * PER_ROUND
        for k in steps:
            at = (z + k) % 8
            total = hb[r, y, at]
            for d in range(1, 4):
                arrive(yb[d - 1].at[r, at], base + Y_RS + (d - 1) * 8 + k, y_dev(d))
                total = total + yb[d - 1][r, at]
            zs[r, at] = total
            if k:
                send(zs.at[r, at], zb.at[r, k - 1], base + Z_RS + k - 1, z_dev(k)[0])

    def scatter_items_total(r):
        base = r * PER_ROUND
        total = zs[r, z]
        for k in NEAR_FIRST:
            arrive(zb.at[r, k - 1], base + Z_RS + k - 1, z_dev(8 - k)[0])
            total = total + zb[r, k - 1]
        return total

    def store_items(r, m, value):
        first = 2 * m % 4
        pi[r, m // 2, first : first + 2] = value.reshape(2, 2, 64, 256)

    def scatter(r):
        if r:
            scatter_users_forward(r, 0)
        scatter_items_y(r)
        scatter_users_forward(r, 1)
        scatter_items_z(r, FAR_FIRST[:3])
        if r:
            scatter_users_sum(r, 0)
        scatter_items_z(r, FAR_FIRST[3:] + (0,))
        users = scatter_users_total(r)
        if r:
            users = gu[...] + users
        else:
            gu[...] = users
        if r < LAYERS:
            gather_users_start(r + 1, users)
        items = scatter_items_total(r)
        if r:
            items = gi[...] + items
        else:
            gi[...] = items
        return users, items

    def send_tiles(first, last):
        for n in range(first, last):
            h = n // 3
            start = (2 * h + 1 - c % 2) * GROUP + n % 3 * PIECE
            send(
                tiles_ref.at[pl.ds(start, PIECE)],
                tbuf[h].at[1, pl.ds(n % 3 * PIECE, PIECE)],
                TILES + n,
                pair_dev,
            )

    def place_tiles(h):
        own_tiles[h].wait()
        for n in range(3 * h, 3 * h + 3):
            arrive(tbuf[h].at[1, pl.ds(n % 3 * PIECE, PIECE)], TILES + n, pair_dev)

        def place(row, carry):
            at_row = pl.ds(pl.multiple_of(h * 512 + row * 128, 128), 128)
            for col in range(8):
                at_col = slice(col * 128, (col + 1) * 128)
                spot = (2 * h + c % 2) * PLACES + row * 8 + col
                tile = tbuf[h][0, sints[c, 4, spot]] + tbuf[h][1, sints[pair, 4, spot]]
                ah[at_row, at_col], al[at_row, at_col] = split2(tile)
                ath[at_col, at_row], atl[at_col, at_row] = split2(tile.T)
            return carry

        lax.fori_loop(0, 4, place, 0)

    to_scalars = pltpu.make_async_copy(gints, sints, lsem.at[2])

    def loss_gradient():
        for k in range(1, 4):
            dev, other = hot_dev(k)
            send(gints.at[c], gints.at[c], INTS + k - 1, dev)
        gather_items_start(0, if_ref[...])
        gather_users_start(0, uf_ref[...])
        send_tiles(0, EARLY)
        gather_items_z(0, NEAR_FIRST[:2])
        gather_users_forward(0)
        for k in range(1, 4):
            dev, other = hot_dev(4 - k)
            arrive(gints.at[other], INTS + k - 1, dev)
        to_scalars.start()
        for h in range(4):
            span = slice(h * 256, (h + 1) * 256)
            buyers = jnp.where(gints[h, 1:2, :] == c, gints[h, 0:1, :], -1)
            rows = lax.broadcasted_iota(jnp.int32, (512, 256), 0)
            ohu[:, span] = jnp.where(rows == buyers, 1.0, 0.0).astype(BF16)
        gather_items_z(0, NEAR_FIRST[2:])
        for h in range(4):
            span = slice(h * 256, (h + 1) * 256)
            rows = lax.broadcasted_iota(jnp.int32, (1024, 256), 0)
            chosen = jnp.where(rows == gints[h, 2:3, :], 1.0, 0.0)
            others = jnp.where(rows == gints[h, 3:4, :], 1.0, 0.0)
            ohd[:, span] = (chosen - others).astype(BF16)
        gather_items_y(0, (0,) + NEAR_FIRST)
        gather_users_end(0)
        ut[0], ut[1], ut[2] = split3(ub[0, slot].reshape(512, 256).T)
        for h in range(4):
            span = slice(h * 256, (h + 1) * 256)
            hot = ohu[:, span]
            buy[:, span] = dot(ut[0], hot) + dot(ut[1], hot) + dot(ut[2], hot)
        gather_items_end(0)
        dt[0], dt[1], dt[2] = split3(ib[0].reshape(1024, 256).T)
        for h in range(4):
            span = slice(h * 256, (h + 1) * 256)
            buyer, signed = buy[:, span], ohd[:, span]
            differ = dot(dt[0], signed) + dot(dt[1], signed) + dot(dt[2], signed)
            margin = jnp.sum(buyer * differ, axis=0, keepdims=True)
            small = jnp.exp(-jnp.abs(margin))
            coef = -jnp.where(margin >= 0, small, 1.0) / (1.0 + small)
            wu[0, :, span], wu[1, :, span] = split2(coef * buyer)
            wd[0, :, span], wd[1, :, span] = split2(coef * differ)
        for m in range(4):
            left = ohd[m * 256 : (m + 1) * 256, :]
            store_items(0, m, dot_nt(left, wu[0]) + dot_nt(left, wu[1]))
        scatter_items_core(0)
        sums = dot_nt(ohu[...], wd[0]) + dot_nt(ohu[...], wd[1])
        pu[0, slot] = sums.reshape(4, 128, 256)
        scatter_users_start(0, 1)
        return scatter(0)

    def layer(r, items):
        gather_items_start(r, items)
        gather_users_over_z(r)
        if r == 1:
            send_tiles(EARLY, PIECES)
            to_scalars.wait()
            place_tiles(0)
        gather_items_z(r, NEAR_FIRST[:2])
        gather_users_forward(r)
        gather_items_z(r, NEAR_FIRST[2:6])
        gather_users_far(r, (0, 1))
        gather_items_z(r, NEAR_FIRST[6:])
        gather_items_y(r, (0,) + NEAR_FIRST[:4])
        gather_users_far(r, (2, 3))
        gather_items_y(r, NEAR_FIRST[4:])
        gather_items_end(r)
        if r == 1:
            place_tiles(1)
        xh, xl = split2(ib[r].reshape(1024, 256))
        for own in range(2):
            place = place_of(own)
            rows = pl.ds(pl.multiple_of(place * 512, 512), 512)
            sums = dot(ah[rows], xh) + dot(ah[rows], xl) + dot(al[rows], xh)
            pu[r, place] = sums.reshape(4, 128, 256)
            scatter_users_start(r, own)
        gather_users_end(r)
        uh, ul = split2(ub[r].reshape(1024, 256))
        for m in range(4):
            rows = slice(m * 256, (m + 1) * 256)
            store_items(r, m, dot(ath[rows], uh) + dot(ath[rows], ul) + dot(atl[rows], uh))
        scatter_items_core(r)
        return scatter(r)

    def rounds():
        users, items = loss_gradient()
        for r in range(1, ROUNDS):
            users, items = layer(r, items)
        return users, items

    users, items = rounds()
    uo_ref[...] = users / (LAYERS + 1.0)
    io_ref[...] = items / (LAYERS + 1.0)
    for copy in started:
        copy.wait_send()


def body(user_final, item_final, tiles, tile_rows, tile_cols, tile_count, triplets):
    slots = tiles.shape[0]
    buyers = triplets[:, 0] % 2048
    chosen = triplets[:, 1] // 256 * 64 + triplets[:, 1] % 64
    others = triplets[:, 2] // 256 * 64 + triplets[:, 2] % 64
    slot = jnp.arange(slots, dtype=jnp.int32)
    spot = slot // GROUP * PLACES + tile_rows // 4 * 8 + tile_cols
    spot = jnp.where(slot < tile_count[0], spot, -1)
    match = spot[None, :] == jnp.arange(4 * PLACES, dtype=jnp.int32)[:, None]
    source = GROUP + jnp.sum(jnp.where(match, slot % GROUP - GROUP, 0), axis=1)
    source = jnp.concatenate([source, source])
    blank = jnp.zeros_like(source)
    ints = jnp.stack(
        [
            buyers // 512 * 128 + buyers % 128,
            buyers // 128 % 4,
            chosen,
            others,
            source,
            blank,
            blank,
            blank,
        ]
    ).astype(jnp.int32)
    vmem = pl.BlockSpec(memory_space=pltpu.VMEM)
    return pl.pallas_call(
        kernel,
        out_shape=(
            jax.ShapeDtypeStruct((128, 256), F32),
            jax.ShapeDtypeStruct((16, 256), F32),
        ),
        in_specs=[vmem, vmem, vmem, pl.BlockSpec(memory_space=pl.ANY)],
        out_specs=(vmem, vmem),
        scratch_shapes=[
            pltpu.VMEM((4, 8, 256), jnp.int32),
            pltpu.SMEM((4, 8, 256), jnp.int32),
            pltpu.VMEM((2, GROUP + 1, 128, 128), F32),
            pltpu.VMEM((2, GROUP + 1, 128, 128), F32),
            pltpu.VMEM((1024, 1024), BF16),
            pltpu.VMEM((1024, 1024), BF16),
            pltpu.VMEM((1024, 1024), BF16),
            pltpu.VMEM((1024, 1024), BF16),
            pltpu.VMEM((512, 1024), BF16),
            pltpu.VMEM((1024, 1024), BF16),
            pltpu.VMEM((256, 1024), F32),
            pltpu.VMEM((3, 256, 512), BF16),
            pltpu.VMEM((3, 256, 1024), BF16),
            pltpu.VMEM((2, 256, 1024), BF16),
            pltpu.VMEM((2, 256, 1024), BF16),
            pltpu.VMEM((ROUNDS, 2, 4, 128, 256), F32),
            pltpu.VMEM((ROUNDS, 2, 4, 2, 4, 16, 256), F32),
            pltpu.VMEM((ROUNDS, 2, 4, 128, 256), F32),
            pltpu.VMEM((ROUNDS, 2, 4, 2, 64, 256), F32),
            pltpu.VMEM((ROUNDS, 2, 128, 256), F32),
            pltpu.VMEM((ROUNDS, 2, 128, 256), F32),
            pltpu.VMEM((ROUNDS, 2, 128, 256), F32),
            pltpu.VMEM((ROUNDS, 128, 256), F32),
            pltpu.VMEM((ROUNDS, 2, 4, 64, 256), F32),
            pltpu.VMEM((ROUNDS, 4, 8, 16, 256), F32),
            pltpu.VMEM((ROUNDS, 8, 16, 256), F32),
            pltpu.VMEM((ROUNDS, 8, 16, 256), F32),
            pltpu.VMEM((ROUNDS, 8, 16, 256), F32),
            pltpu.VMEM((ROUNDS, 8, 16, 256), F32),
            pltpu.VMEM((ROUNDS, 7, 16, 256), F32),
            pltpu.VMEM((128, 256), F32),
            pltpu.VMEM((16, 256), F32),
            pltpu.SemaphoreType.DMA((COPIES,)),
            pltpu.SemaphoreType.DMA((COPIES,)),
            pltpu.SemaphoreType.DMA((3,)),
        ],
        compiler_params=pltpu.CompilerParams(
            collective_id=0, has_side_effects=True, vmem_limit_bytes=52 * 1024 * 1024
        ),
        name="propagate",
    )(ints, user_final, item_final, tiles)


def solution(mesh):
    placed = (
        P(("user", "item", "hot"), None),
        P(("user", "item", "hot"), None),
        P(("user", "item", "hot"), None, None),
        P(("user", "item", "hot")),
        P(("user", "item", "hot")),
        P(("user", "item", "hot")),
        P(("user", "item", "hot"), None),
    )
    return jax.shard_map(
        body,
        mesh=mesh,
        in_specs=placed,
        out_specs=(P(("user", "item", "hot"), None), P(("user", "item", "hot"), None)),
        check_vma=False,
    )
```

```python
import jax
import jax.numpy as jnp
from jax import lax
from jax.experimental import pallas as pl
from jax.experimental.pallas import tpu as pltpu
from jax.sharding import PartitionSpec as P

MESH = pl.DeviceIdType.MESH
F32 = jnp.float32
BF16 = jnp.bfloat16
LAYERS = 2


ROUNDS = LAYERS + 1
GROUP = 12
PLACES = 32

CHUNKS = 4
CHUNK = 32
PIECES = 6
PIECE = 4
EARLY = 4

U_AG = 0
Z_AG = U_AG + 7 * CHUNKS
Y_AG = Z_AG + 7
C_AG = Y_AG + 24
C_RS = C_AG + 32
Y_RS = C_RS + 4
Z_RS = Y_RS + 24
U_RS = Z_RS + 7
PER_ROUND = U_RS + 7 * CHUNKS
INTS = PER_ROUND * ROUNDS
TILES = INTS + 3
COPIES = TILES + PIECES
NEAR_FIRST = (1, 7, 2, 6, 3, 5, 4)
FAR_FIRST = (4, 5, 3, 6, 2, 7, 1)


def split2(x):
    hi = x.astype(BF16)
    return hi, (x - hi.astype(F32)).astype(BF16)


def split3(x):
    hi = x.astype(BF16)
    rest = x - hi.astype(F32)
    mid = rest.astype(BF16)
    return hi, mid, (rest - mid.astype(F32)).astype(BF16)


def dot(a, b):
    return jnp.dot(a, b, preferred_element_type=F32)


def dot_nt(a, b):
    return lax.dot_general(a, b, (((1,), (1,)), ((), ())), preferred_element_type=F32)


def kernel(
    trip_ref,
    rows_ref,
    cols_ref,
    count_ref,
    uf_ref,
    if_ref,
    tiles_ref,
    uo_ref,
    io_ref,
    trips,
    gints,
    sints,
    tbuf0,
    tbuf1,
    ah,
    al,
    ath,
    atl,
    ohu,
    ohd,
    buy,
    ut,
    dt,
    wd,
    wu,
    ub,
    ib,
    pu,
    pi,
    um,
    ua,
    uz,
    uq,
    rc,
    hb,
    ym,
    ya,
    yz,
    zs,
    zb,
    gu,
    gi,
    ssem,
    rsem,
    lsem,
):
    a = lax.axis_index("user")
    b = lax.axis_index("item")
    c = lax.axis_index("hot")
    core = a % 2
    y = (a // 2) % 4
    zhi = a // 8
    z = zhi * 4 + c

    def user_index(zhi_, y_, core_):
        return (zhi_ * 4 + y_) * 2 + core_

    def ring(v):
        even = v + 1 - 2 * (v % 2)
        odd = 3 - v
        first = (1 - core) * even + core * odd
        second = (1 - core) * odd + core * even
        return first, second, (v + 2) % 4

    x1, x2, xo = ring(b)
    xa_dev = (a, x1, c)
    xb_dev = (a, x2, c)
    xo_dev = (a, xo, c)
    tbuf = (tbuf0, tbuf1)
    yb = (ym, ya, yz)
    slot = c // 2
    pair = c + 1 - 2 * (c % 2)
    from_pair = 3 - 2 * (c % 2)
    pair_dev = (a, b, pair)
    far_dev = (a, b, (c + 2) % 4)
    sib = (user_index(zhi, y, 1 - core), b, c)

    def z_dev(k):
        other = (z + k) % 8
        return (user_index(other // 4, y, core), b, other % 4), other // 4, other % 4

    def y_dev(k):
        other = (y + k) % 4
        return (user_index(zhi, other, core), b, c)

    def hot_dev(k):
        other = (c + k) % 4
        return (a, b, other), other

    started = []

    def send(src, dst, index, dev):
        copy = pltpu.make_async_remote_copy(
            src_ref=src,
            dst_ref=dst,
            send_sem=ssem.at[index],
            recv_sem=rsem.at[index],
            device_id=dev,
            device_id_type=MESH,
        )
        copy.start()
        started.append(copy)

    def arrive(dst, index, dev):
        pltpu.make_async_remote_copy(
            src_ref=dst,
            dst_ref=dst,
            send_sem=ssem.at[index],
            recv_sem=rsem.at[index],
            device_id=dev,
            device_id_type=MESH,
        ).wait_recv()

    barrier = pltpu.get_barrier_semaphore()
    peers = [xa_dev, xb_dev, xo_dev, sib]
    peers += [y_dev(k) for k in range(1, 4)] + [z_dev(k)[0] for k in range(1, 8)]
    for dev in peers:
        pl.semaphore_signal(barrier, inc=1, device_id=dev, device_id_type=MESH)
    own_tiles = [
        pltpu.make_async_copy(
            tiles_ref.at[pl.ds((2 * h + c % 2) * GROUP, GROUP)],
            tbuf[h].at[0, pl.ds(0, GROUP)],
            lsem.at[h],
        )
        for h in range(2)
    ]
    for copy in own_tiles:
        copy.start()
    shares = [
        pltpu.make_async_copy(trip_ref, trips, lsem.at[3]),
        pltpu.make_async_copy(uf_ref, ub.at[0, slot, b], lsem.at[4]),
        pltpu.make_async_copy(if_ref, ib.at[0, zhi, y, core, c], lsem.at[5]),
    ]
    for copy in shares:
        copy.start()
    for h in range(2):
        tbuf[h][0, GROUP] = jnp.zeros((128, 128), F32)
        tbuf[h][1, GROUP] = jnp.zeros((128, 128), F32)
    for copy in shares:
        copy.wait()
    lanes = lax.broadcasted_iota(jnp.int32, (1, 128), 1)
    source = jnp.full((1, 128), GROUP, jnp.int32)
    for n in range(4 * GROUP):
        spot = n // GROUP * PLACES + rows_ref[n] // 4 * 8 + cols_ref[n]
        spot = jnp.where(n < count_ref[0], spot, -1)
        source = jnp.where(lanes == spot, n % GROUP, source)
    own = trips[...].T
    buyers = own[0:1] % 2048
    gints[0, 0:1] = buyers // 512 * 128 + buyers % 128
    gints[0, 1:2] = buyers // 128 % 4
    gints[0, 2:3] = own[1:2] // 256 * 64 + own[1:2] % 64
    gints[0, 3:4] = own[2:3] // 256 * 64 + own[2:3] % 64
    gints[0, 4:5, 0:128] = source
    gints[0, 4:5, 128:256] = source
    gints[0, 5:8] = jnp.zeros((3, 256), jnp.int32)
    count_up = lax.broadcasted_iota(jnp.int32, (256, 256), 0).astype(F32).astype(BF16)

    def one_hot(index, m):
        inside = jnp.where(index // 256 == m, index % 256, -1).astype(F32)
        inside = jnp.broadcast_to(inside, (256, 256)).astype(BF16)
        return jnp.where(count_up == inside, jnp.ones((), BF16), jnp.zeros((), BF16))

    def select_users(k):
        buyers = jnp.where(gints[k, 1:2, :] == c, gints[k, 0:1, :], -1)
        for m in range(2):
            ohu[m * 256 : (m + 1) * 256, k * 256 : (k + 1) * 256] = one_hot(buyers, m)

    def select_items(k):
        for m in range(4):
            signed = one_hot(gints[k, 2:3, :], m) - one_hot(gints[k, 3:4, :], m)
            ohd[m * 256 : (m + 1) * 256, k * 256 : (k + 1) * 256] = signed

    select_users(0)
    select_items(0)
    pl.semaphore_wait(barrier, len(peers))

    def chunk(q):
        return pl.ds(q * CHUNK, CHUNK)

    def place_of(own):
        return slot if own else 1 - slot

    def along_z(k):
        other = (z + k) % 8
        return other // 4, other % 4

    def gather_users_start(r, users):
        base = r * PER_ROUND + U_AG
        if r:
            ub[r, slot, b] = users
        for q in range(CHUNKS):
            mine = ub.at[r, slot, b, chunk(q)]
            send(mine, mine, base + q, xa_dev)
            send(mine, mine, base + CHUNKS + q, xb_dev)

    def gather_users_over_z(r):
        for q in range(CHUNKS):
            mine = ub.at[r, slot, b, chunk(q)]
            send(mine, mine, r * PER_ROUND + U_AG + 6 * CHUNKS + q, far_dev)

    def gather_users_far(r, chunks):
        base = r * PER_ROUND + U_AG
        for q in chunks:
            other = ub.at[r, 1 - slot, b, chunk(q)]
            arrive(other, base + 6 * CHUNKS + q, far_dev)
            send(other, other, base + 5 * CHUNKS + q, xo_dev)
            send(other, other, base + 3 * CHUNKS + q, xa_dev)
            send(other, other, base + 4 * CHUNKS + q, xb_dev)

    def gather_users_forward(r):
        base = r * PER_ROUND + U_AG
        for q in range(CHUNKS):
            block = ub.at[r, slot, x1, chunk(q)]
            arrive(block, base + q, xa_dev)
            send(block, block, base + 2 * CHUNKS + q, xb_dev)

    def gather_users_end(r):
        base = r * PER_ROUND + U_AG
        for q in range(CHUNKS):
            arrive(ub.at[r, slot, x2, chunk(q)], base + CHUNKS + q, xb_dev)
        for q in range(CHUNKS):
            arrive(ub.at[r, slot, xo, chunk(q)], base + 2 * CHUNKS + q, xb_dev)
        if r:
            base = base + 3 * CHUNKS
            for q in range(CHUNKS):
                arrive(ub.at[r, 1 - slot, x1, chunk(q)], base + q, xa_dev)
                arrive(ub.at[r, 1 - slot, x2, chunk(q)], base + CHUNKS + q, xb_dev)
                arrive(ub.at[r, 1 - slot, xo, chunk(q)], base + 2 * CHUNKS + q, xo_dev)

    def scatter_users_start(r, own):
        base = r * PER_ROUND + U_RS + 3 * CHUNKS * own
        place = place_of(own)
        for q in range(CHUNKS):
            send(pu.at[r, place, xo, chunk(q)], um.at[r, own, chunk(q)], base + q, xb_dev)
        for q in range(CHUNKS):
            send(pu.at[r, place, x2, chunk(q)], uz.at[r, own, chunk(q)], base + CHUNKS + q, xb_dev)

    def scatter_users_forward(r, own):
        base = r * PER_ROUND + U_RS + 3 * CHUNKS * own
        place = place_of(own)
        for q in range(CHUNKS):
            arrive(um.at[r, own, chunk(q)], base + q, xb_dev)
            pu[r, place, x1, chunk(q)] = pu[r, place, x1, chunk(q)] + um[r, own, chunk(q)]
            sums = pu.at[r, place, x1, chunk(q)]
            send(sums, ua.at[r, own, chunk(q)], base + 2 * CHUNKS + q, xa_dev)

    def scatter_users_sum(r, own):
        base = r * PER_ROUND + U_RS + 3 * CHUNKS * own
        place = place_of(own)
        for q in range(CHUNKS):
            arrive(uz.at[r, own, chunk(q)], base + CHUNKS + q, xb_dev)
            arrive(ua.at[r, own, chunk(q)], base + 2 * CHUNKS + q, xa_dev)
            sums = pu[r, place, b, chunk(q)] + uz[r, own, chunk(q)] + ua[r, own, chunk(q)]
            pu[r, place, b, chunk(q)] = sums
            if not own:
                index = r * PER_ROUND + U_RS + 6 * CHUNKS + q
                send(pu.at[r, place, b, chunk(q)], uq.at[r, chunk(q)], index, far_dev)

    def scatter_users_total(r):
        scatter_users_sum(r, 1)
        total = pu[r, slot, b]
        if r:
            for q in range(CHUNKS):
                arrive(uq.at[r, chunk(q)], r * PER_ROUND + U_RS + 6 * CHUNKS + q, far_dev)
            total = total + uq[r]
        return total

    def gather_items_start(r, items):
        base = r * PER_ROUND
        if r:
            ib[r, zhi, y, core, c] = items
        mine = ib.at[r, zhi, y, core, c]
        for k in FAR_FIRST:
            send(mine, mine, base + Z_AG + k - 1, z_dev(k)[0])
        pass_on(r, 0)

    def pass_on(r, k):
        base = r * PER_ROUND
        hi, lo = along_z(k)
        piece = ib.at[r, hi, y, core, lo]
        for d in (2, 1, 3):
            send(piece, piece, base + Y_AG + (d - 1) * 8 + k, y_dev(d))
        send(piece, piece, base + C_AG + k, sib)

    def gather_items_z(r, steps):
        base = r * PER_ROUND
        for k in steps:
            hi, lo = along_z(k)
            arrive(ib.at[r, hi, y, core, lo], base + Z_AG + (8 - k) - 1, z_dev(k)[0])
            pass_on(r, k)

    def gather_items_y(r, steps):
        base = r * PER_ROUND
        for k in steps:
            hi, lo = along_z(k)
            for d in (1, 3, 2):
                piece = ib.at[r, hi, (y + d) % 4, core, lo]
                arrive(piece, base + Y_AG + (3 - d) * 8 + k, y_dev(d))
                send(piece, piece, base + C_AG + d * 8 + k, sib)

    def gather_items_end(r):
        base = r * PER_ROUND
        for k in (0,) + NEAR_FIRST:
            hi, lo = along_z(k)
            for d in range(4):
                piece = ib.at[r, hi, (y + d) % 4, 1 - core, lo]
                arrive(piece, base + C_AG + d * 8 + k, sib)

    def scatter_items_core(r):
        base = r * PER_ROUND
        for d in (2, 1, 3, 0):
            other = (y + d) % 4
            send(pi.at[r, :, other, 1 - core], rc.at[r, :, other], base + C_RS + d, sib)

    def scatter_items_y(r):
        base = r * PER_ROUND
        for d in (2, 1, 3, 0):
            other = (y + d) % 4
            arrive(rc.at[r, :, other], base + C_RS + d, sib)
            sums = pi[r, :, other, core] + rc[r, :, other]
            hb[r, other] = sums.reshape(8, 16, 256)
        for k in FAR_FIRST + (0,):
            at = (z + k) % 8
            for d in (2, 1, 3):
                source = hb.at[r, (y + d) % 4, at]
                send(source, yb[d - 1].at[r, at], base + Y_RS + (d - 1) * 8 + k, y_dev(d))

    def scatter_items_z(r, steps):
        base = r * PER_ROUND
        for k in steps:
            at = (z + k) % 8
            total = hb[r, y, at]
            for d in range(1, 4):
                arrive(yb[d - 1].at[r, at], base + Y_RS + (d - 1) * 8 + k, y_dev(d))
                total = total + yb[d - 1][r, at]
            zs[r, at] = total
            if k:
                send(zs.at[r, at], zb.at[r, k - 1], base + Z_RS + k - 1, z_dev(k)[0])

    def scatter_items_total(r):
        base = r * PER_ROUND
        total = zs[r, z]
        for k in NEAR_FIRST:
            arrive(zb.at[r, k - 1], base + Z_RS + k - 1, z_dev(8 - k)[0])
            total = total + zb[r, k - 1]
        return total

    def store_items(r, m, value):
        first = 2 * m % 4
        pi[r, m // 2, first : first + 2] = value.reshape(2, 2, 64, 256)

    def scatter(r):
        if r:
            scatter_users_forward(r, 0)
        scatter_items_y(r)
        scatter_users_forward(r, 1)
        if r == 0:
            to_scalars.wait()
            place_tiles(0)
        scatter_items_z(r, FAR_FIRST[:3])
        if r:
            scatter_users_sum(r, 0)
        scatter_items_z(r, FAR_FIRST[3:] + (0,))
        if r == 0:
            send_tiles(EARLY, EARLY + 1)
        users = scatter_users_total(r)
        if r:
            users = gu[...] + users
        else:
            gu[...] = users
        if r < LAYERS:
            gather_users_start(r + 1, users)
        items = scatter_items_total(r)
        if r:
            items = gi[...] + items
        else:
            gi[...] = items
        return users, items

    def send_tiles(first, last):
        for n in range(first, last):
            h = n // 3
            start = (2 * h + 1 - c % 2) * GROUP + n % 3 * PIECE
            send(
                tiles_ref.at[pl.ds(start, PIECE)],
                tbuf[h].at[1, pl.ds(n % 3 * PIECE, PIECE)],
                TILES + n,
                pair_dev,
            )

    def place_tiles(h):
        own_tiles[h].wait()
        for n in range(3 * h, 3 * h + 3):
            arrive(tbuf[h].at[1, pl.ds(n % 3 * PIECE, PIECE)], TILES + n, pair_dev)

        def place(row, carry):
            at_row = pl.ds(pl.multiple_of(h * 512 + row * 128, 128), 128)
            for col in range(8):
                at_col = slice(col * 128, (col + 1) * 128)
                spot = (2 * h + c % 2) * PLACES + row * 8 + col
                tile = tbuf[h][0, sints[0, 4, spot]] + tbuf[h][1, sints[from_pair, 4, spot]]
                ah[at_row, at_col], al[at_row, at_col] = split2(tile)
                ath[at_col, at_row], atl[at_col, at_row] = split2(tile.T)
            return carry

        lax.fori_loop(0, 4, place, 0)

    to_scalars = pltpu.make_async_copy(gints, sints, lsem.at[2])

    def loss_gradient():
        for k in range(1, 4):
            dev, other = hot_dev(k)
            send(gints.at[0], gints.at[k], INTS + k - 1, dev)
        gather_items_start(0, None)
        gather_users_start(0, None)
        send_tiles(0, EARLY)
        gather_items_z(0, NEAR_FIRST[:2])
        gather_users_forward(0)
        for k in range(1, 4):
            arrive(gints.at[k], INTS + k - 1, hot_dev(4 - k)[0])
        to_scalars.start()
        gather_items_z(0, NEAR_FIRST[2:])
        for k in range(1, 4):
            select_users(k)
        gather_items_y(0, (0,) + NEAR_FIRST[:4])
        for k in range(1, 4):
            select_items(k)
        gather_items_y(0, NEAR_FIRST[4:])
        gather_users_end(0)
        ut[0], ut[1], ut[2] = split3(ub[0, slot].reshape(512, 256).T)
        for h in range(4):
            span = slice(h * 256, (h + 1) * 256)
            hot = ohu[:, span]
            buy[:, span] = dot(ut[0], hot) + dot(ut[1], hot) + dot(ut[2], hot)
        gather_items_end(0)
        dt[0], dt[1], dt[2] = split3(ib[0].reshape(1024, 256).T)
        for h in range(4):
            span = slice(h * 256, (h + 1) * 256)
            buyer, signed = buy[:, span], ohd[:, span]
            differ = dot(dt[0], signed) + dot(dt[1], signed) + dot(dt[2], signed)
            margin = jnp.sum(buyer * differ, axis=0, keepdims=True)
            small = jnp.exp(-jnp.abs(margin))
            coef = -jnp.where(margin >= 0, small, 1.0) / (1.0 + small)
            wu[0, :, span], wu[1, :, span] = split2(coef * buyer)
            wd[0, :, span], wd[1, :, span] = split2(coef * differ)
        for m in range(4):
            left = ohd[m * 256 : (m + 1) * 256, :]
            store_items(0, m, dot_nt(left, wu[0]) + dot_nt(left, wu[1]))
        scatter_items_core(0)
        sums = dot_nt(ohu[...], wd[0]) + dot_nt(ohu[...], wd[1])
        pu[0, slot] = sums.reshape(4, 128, 256)
        scatter_users_start(0, 1)
        return scatter(0)

    def layer(r, items):
        gather_items_start(r, items)
        gather_users_over_z(r)
        if r == 1:
            send_tiles(EARLY + 1, PIECES)
        gather_items_z(r, NEAR_FIRST[:2])
        gather_users_forward(r)
        gather_items_z(r, NEAR_FIRST[2:6])
        gather_users_far(r, (0, 1))
        gather_items_z(r, NEAR_FIRST[6:])
        gather_items_y(r, (0,) + NEAR_FIRST[:4])
        gather_users_far(r, (2, 3))
        gather_items_y(r, NEAR_FIRST[4:])
        gather_items_end(r)
        if r == 1:
            place_tiles(1)
        xh, xl = split2(ib[r].reshape(1024, 256))
        for own in range(2):
            place = place_of(own)
            rows = pl.ds(pl.multiple_of(place * 512, 512), 512)
            sums = dot(ah[rows], xh) + dot(ah[rows], xl) + dot(al[rows], xh)
            pu[r, place] = sums.reshape(4, 128, 256)
            scatter_users_start(r, own)
        gather_users_end(r)
        uh, ul = split2(ub[r].reshape(1024, 256))
        for m in range(4):
            rows = slice(m * 256, (m + 1) * 256)
            store_items(r, m, dot(ath[rows], uh) + dot(ath[rows], ul) + dot(atl[rows], uh))
        scatter_items_core(r)
        return scatter(r)

    def rounds():
        users, items = loss_gradient()
        for r in range(1, ROUNDS):
            users, items = layer(r, items)
        return users, items

    users, items = rounds()
    uo_ref[...] = users / (LAYERS + 1.0)
    io_ref[...] = items / (LAYERS + 1.0)
    for copy in started:
        copy.wait_send()


def body(user_final, item_final, tiles, tile_rows, tile_cols, tile_count, triplets):
    vmem = pl.BlockSpec(memory_space=pltpu.VMEM)
    smem = pl.BlockSpec(memory_space=pltpu.SMEM)
    anywhere = pl.BlockSpec(memory_space=pl.ANY)
    return pl.pallas_call(
        kernel,
        out_shape=(
            jax.ShapeDtypeStruct((128, 256), F32),
            jax.ShapeDtypeStruct((16, 256), F32),
        ),
        in_specs=[anywhere, smem, smem, smem, anywhere, anywhere, anywhere],
        out_specs=(vmem, vmem),
        scratch_shapes=[
            pltpu.VMEM((256, 3), jnp.int32),
            pltpu.VMEM((4, 8, 256), jnp.int32),
            pltpu.SMEM((4, 8, 256), jnp.int32),
            pltpu.VMEM((2, GROUP + 1, 128, 128), F32),
            pltpu.VMEM((2, GROUP + 1, 128, 128), F32),
            pltpu.VMEM((1024, 1024), BF16),
            pltpu.VMEM((1024, 1024), BF16),
            pltpu.VMEM((1024, 1024), BF16),
            pltpu.VMEM((1024, 1024), BF16),
            pltpu.VMEM((512, 1024), BF16),
            pltpu.VMEM((1024, 1024), BF16),
            pltpu.VMEM((256, 1024), F32),
            pltpu.VMEM((3, 256, 512), BF16),
            pltpu.VMEM((3, 256, 1024), BF16),
            pltpu.VMEM((2, 256, 1024), BF16),
            pltpu.VMEM((2, 256, 1024), BF16),
            pltpu.VMEM((ROUNDS, 2, 4, 128, 256), F32),
            pltpu.VMEM((ROUNDS, 2, 4, 2, 4, 16, 256), F32),
            pltpu.VMEM((ROUNDS, 2, 4, 128, 256), F32),
            pltpu.VMEM((ROUNDS, 2, 4, 2, 64, 256), F32),
            pltpu.VMEM((ROUNDS, 2, 128, 256), F32),
            pltpu.VMEM((ROUNDS, 2, 128, 256), F32),
            pltpu.VMEM((ROUNDS, 2, 128, 256), F32),
            pltpu.VMEM((ROUNDS, 128, 256), F32),
            pltpu.VMEM((ROUNDS, 2, 4, 64, 256), F32),
            pltpu.VMEM((ROUNDS, 4, 8, 16, 256), F32),
            pltpu.VMEM((ROUNDS, 8, 16, 256), F32),
            pltpu.VMEM((ROUNDS, 8, 16, 256), F32),
            pltpu.VMEM((ROUNDS, 8, 16, 256), F32),
            pltpu.VMEM((ROUNDS, 8, 16, 256), F32),
            pltpu.VMEM((ROUNDS, 7, 16, 256), F32),
            pltpu.VMEM((128, 256), F32),
            pltpu.VMEM((16, 256), F32),
            pltpu.SemaphoreType.DMA((COPIES,)),
            pltpu.SemaphoreType.DMA((COPIES,)),
            pltpu.SemaphoreType.DMA((6,)),
        ],
        compiler_params=pltpu.CompilerParams(
            collective_id=0, has_side_effects=True, vmem_limit_bytes=52 * 1024 * 1024
        ),
        name="propagate",
    )(triplets, tile_rows, tile_cols, tile_count, user_final, item_final, tiles)


def solution(mesh):
    placed = (
        P(("user", "item", "hot"), None),
        P(("user", "item", "hot"), None),
        P(("user", "item", "hot"), None, None),
        P(("user", "item", "hot")),
        P(("user", "item", "hot")),
        P(("user", "item", "hot")),
        P(("user", "item", "hot"), None),
    )
    return jax.shard_map(
        body,
        mesh=mesh,
        in_specs=placed,
        out_specs=(P(("user", "item", "hot"), None), P(("user", "item", "hot"), None)),
        check_vma=False,
    )
```

```python
import jax
import jax.numpy as jnp
from jax import lax
from jax.experimental import pallas as pl
from jax.experimental.pallas import tpu as pltpu
from jax.sharding import PartitionSpec as P

MESH = pl.DeviceIdType.MESH
F32 = jnp.float32
BF16 = jnp.bfloat16
LAYERS = 2


ROUNDS = LAYERS + 1
GROUP = 12
PLACES = 32

CHUNKS = 4
CHUNK = 32
PIECES = 6
PIECE = 4
EARLY = 4

U_AG = 0
Z_AG = U_AG + 7 * CHUNKS
Y_AG = Z_AG + 7
C_AG = Y_AG + 24
C_RS = C_AG + 32
Y_RS = C_RS + 4
Z_RS = Y_RS + 24
U_RS = Z_RS + 7
PER_ROUND = U_RS + 7 * CHUNKS
INTS = PER_ROUND * ROUNDS
SOURCE = INTS + 3
TILES = SOURCE + 1
COPIES = TILES + PIECES
NEAR_FIRST = (1, 7, 2, 6, 3, 5, 4)
FAR_FIRST = (4, 5, 3, 6, 2, 7, 1)


def split2(x):
    hi = x.astype(BF16)
    return hi, (x - hi.astype(F32)).astype(BF16)


def split3(x):
    hi = x.astype(BF16)
    rest = x - hi.astype(F32)
    mid = rest.astype(BF16)
    return hi, mid, (rest - mid.astype(F32)).astype(BF16)


def dot(a, b):
    return jnp.dot(a, b, preferred_element_type=F32)


def kernel(
    trip_ref,
    spot_ref,
    uf_ref,
    if_ref,
    tiles_ref,
    uo_ref,
    io_ref,
    gints,
    gsource,
    sints,
    tbuf0,
    tbuf1,
    ah,
    al,
    ath,
    atl,
    ohu,
    ohd,
    uho,
    dho,
    buy,
    ut,
    dt,
    wd,
    wu,
    ub,
    ib,
    pu,
    pi,
    um,
    ua,
    uz,
    uq,
    rc,
    hb,
    ym,
    ya,
    yz,
    zs,
    zb,
    gu,
    gi,
    ssem,
    rsem,
    lsem,
):
    a = lax.axis_index("user")
    b = lax.axis_index("item")
    c = lax.axis_index("hot")
    core = a % 2
    y = (a // 2) % 4
    zhi = a // 8
    z = zhi * 4 + c

    def user_index(zhi_, y_, core_):
        return (zhi_ * 4 + y_) * 2 + core_

    def ring(v):
        even = v + 1 - 2 * (v % 2)
        odd = 3 - v
        first = (1 - core) * even + core * odd
        second = (1 - core) * odd + core * even
        return first, second, (v + 2) % 4

    x1, x2, xo = ring(b)
    xa_dev = (a, x1, c)
    xb_dev = (a, x2, c)
    xo_dev = (a, xo, c)
    tbuf = (tbuf0, tbuf1)
    yb = (ym, ya, yz)
    slot = c // 2
    pair = c + 1 - 2 * (c % 2)
    pair_dev = (a, b, pair)
    far_dev = (a, b, (c + 2) % 4)
    sib = (user_index(zhi, y, 1 - core), b, c)

    def z_dev(k):
        other = (z + k) % 8
        return (user_index(other // 4, y, core), b, other % 4), other // 4, other % 4

    def y_dev(k):
        other = (y + k) % 4
        return (user_index(zhi, other, core), b, c)

    def hot_dev(k):
        other = (c + k) % 4
        return (a, b, other), other

    started = []

    def send(src, dst, index, dev):
        copy = pltpu.make_async_remote_copy(
            src_ref=src,
            dst_ref=dst,
            send_sem=ssem.at[index],
            recv_sem=rsem.at[index],
            device_id=dev,
            device_id_type=MESH,
        )
        copy.start()
        started.append(copy)

    def arrive(dst, index, dev):
        pltpu.make_async_remote_copy(
            src_ref=dst,
            dst_ref=dst,
            send_sem=ssem.at[index],
            recv_sem=rsem.at[index],
            device_id=dev,
            device_id_type=MESH,
        ).wait_recv()

    barrier = pltpu.get_barrier_semaphore()
    peers = [xa_dev, xb_dev, xo_dev, sib]
    peers += [y_dev(k) for k in range(1, 4)] + [z_dev(k)[0] for k in range(1, 8)]
    for dev in peers:
        pl.semaphore_signal(barrier, inc=1, device_id=dev, device_id_type=MESH)
    own_tiles = [
        pltpu.make_async_copy(
            tiles_ref.at[pl.ds((2 * h + c % 2) * GROUP, GROUP)],
            tbuf[h].at[0, pl.ds(0, GROUP)],
            lsem.at[h],
        )
        for h in range(2)
    ]
    for copy in own_tiles:
        copy.start()
    shares = [
        pltpu.make_async_copy(uf_ref, ub.at[0, slot, b], lsem.at[4]),
        pltpu.make_async_copy(if_ref, ib.at[0, zhi, y, core, c], lsem.at[5]),
    ]
    for copy in shares:
        copy.start()
    for h in range(2):
        tbuf[h][0, GROUP] = jnp.zeros((128, 128), F32)
        tbuf[h][1, GROUP] = jnp.zeros((128, 128), F32)
    for copy in shares:
        copy.wait()
    lanes = lax.broadcasted_iota(jnp.int32, (1, 128), 1)
    source = jnp.full((1, 128), GROUP, jnp.int32)
    for n in range(4 * GROUP):
        source = jnp.where(lanes == spot_ref[n], n % GROUP, source)
    gsource[0] = source
    buyers = trip_ref[0:1] % 2048
    gints[0, 0:1] = buyers // 512 * 128 + buyers % 128
    gints[0, 1:2] = buyers // 128 % 4
    gints[0, 2:3] = trip_ref[1:2] // 256 * 64 + trip_ref[1:2] % 64
    gints[0, 3:4] = trip_ref[2:3] // 256 * 64 + trip_ref[2:3] % 64
    gints[0, 4:8] = jnp.zeros((4, 256), jnp.int32)
    count_up = lax.broadcasted_iota(jnp.int32, (256, 256), 0).astype(F32).astype(BF16)

    def one_hot(index, m):
        inside = jnp.where(index // 256 == m, index % 256, -1).astype(F32)
        inside = jnp.broadcast_to(inside, (256, 256)).astype(BF16)
        return jnp.where(count_up == inside, jnp.ones((), BF16), jnp.zeros((), BF16))

    count_right = lax.broadcasted_iota(jnp.int32, (256, 256), 1).astype(F32).astype(BF16)

    def one_hot_rows(index, m):
        inside = jnp.where(index // 256 == m, index % 256, -1).astype(F32)
        inside = jnp.broadcast_to(inside, (256, 256)).astype(BF16)
        return jnp.where(count_right == inside, jnp.ones((), BF16), jnp.zeros((), BF16))

    def select_users(k):
        buyers = jnp.where(gints[k, 1:2, :] == c, gints[k, 0:1, :], -1)
        columns = gints[k].T
        column = jnp.where(columns[:, 1:2] == c, columns[:, 0:1], -1)
        for m in range(2):
            block = slice(m * 256, (m + 1) * 256)
            span = slice(k * 256, (k + 1) * 256)
            ohu[block, span] = one_hot(buyers, m)
            uho[span, block] = one_hot_rows(column, m)

    def select_items(k):
        columns = gints[k].T
        for m in range(4):
            block = slice(m * 256, (m + 1) * 256)
            span = slice(k * 256, (k + 1) * 256)
            ohd[block, span] = one_hot(gints[k, 2:3, :], m) - one_hot(gints[k, 3:4, :], m)
            chosen = one_hot_rows(columns[:, 2:3], m)
            dho[span, block] = chosen - one_hot_rows(columns[:, 3:4], m)

    select_users(0)
    select_items(0)
    pl.semaphore_wait(barrier, len(peers))

    def chunk(q):
        return pl.ds(q * CHUNK, CHUNK)

    def place_of(own):
        return slot if own else 1 - slot

    def along_z(k):
        other = (z + k) % 8
        return other // 4, other % 4

    def gather_users_start(r, users):
        base = r * PER_ROUND + U_AG
        if r:
            ub[r, slot, b] = users
        for q in range(CHUNKS):
            mine = ub.at[r, slot, b, chunk(q)]
            send(mine, mine, base + q, xa_dev)
            send(mine, mine, base + CHUNKS + q, xb_dev)

    def gather_users_over_z(r):
        for q in range(CHUNKS):
            mine = ub.at[r, slot, b, chunk(q)]
            send(mine, mine, r * PER_ROUND + U_AG + 6 * CHUNKS + q, far_dev)

    def gather_users_far(r, chunks):
        base = r * PER_ROUND + U_AG
        for q in chunks:
            other = ub.at[r, 1 - slot, b, chunk(q)]
            arrive(other, base + 6 * CHUNKS + q, far_dev)
            send(other, other, base + 5 * CHUNKS + q, xo_dev)
            send(other, other, base + 3 * CHUNKS + q, xa_dev)
            send(other, other, base + 4 * CHUNKS + q, xb_dev)

    def gather_users_forward(r):
        base = r * PER_ROUND + U_AG
        for q in range(CHUNKS):
            block = ub.at[r, slot, x1, chunk(q)]
            arrive(block, base + q, xa_dev)
            send(block, block, base + 2 * CHUNKS + q, xb_dev)

    def gather_users_end(r):
        base = r * PER_ROUND + U_AG
        for q in range(CHUNKS):
            arrive(ub.at[r, slot, x2, chunk(q)], base + CHUNKS + q, xb_dev)
        for q in range(CHUNKS):
            arrive(ub.at[r, slot, xo, chunk(q)], base + 2 * CHUNKS + q, xb_dev)
        if r:
            base = base + 3 * CHUNKS
            for q in range(CHUNKS):
                arrive(ub.at[r, 1 - slot, x1, chunk(q)], base + q, xa_dev)
                arrive(ub.at[r, 1 - slot, x2, chunk(q)], base + CHUNKS + q, xb_dev)
                arrive(ub.at[r, 1 - slot, xo, chunk(q)], base + 2 * CHUNKS + q, xo_dev)

    def scatter_users_start(r, own):
        base = r * PER_ROUND + U_RS + 3 * CHUNKS * own
        place = place_of(own)
        for q in range(CHUNKS):
            send(pu.at[r, place, xo, chunk(q)], um.at[r, own, chunk(q)], base + q, xb_dev)
        for q in range(CHUNKS):
            send(pu.at[r, place, x2, chunk(q)], uz.at[r, own, chunk(q)], base + CHUNKS + q, xb_dev)

    def scatter_users_forward(r, own):
        base = r * PER_ROUND + U_RS + 3 * CHUNKS * own
        place = place_of(own)
        for q in range(CHUNKS):
            arrive(um.at[r, own, chunk(q)], base + q, xb_dev)
            pu[r, place, x1, chunk(q)] = pu[r, place, x1, chunk(q)] + um[r, own, chunk(q)]
            sums = pu.at[r, place, x1, chunk(q)]
            send(sums, ua.at[r, own, chunk(q)], base + 2 * CHUNKS + q, xa_dev)

    def scatter_users_sum(r, own):
        base = r * PER_ROUND + U_RS + 3 * CHUNKS * own
        place = place_of(own)
        for q in range(CHUNKS):
            arrive(uz.at[r, own, chunk(q)], base + CHUNKS + q, xb_dev)
            arrive(ua.at[r, own, chunk(q)], base + 2 * CHUNKS + q, xa_dev)
            sums = pu[r, place, b, chunk(q)] + uz[r, own, chunk(q)] + ua[r, own, chunk(q)]
            pu[r, place, b, chunk(q)] = sums
            if not own:
                index = r * PER_ROUND + U_RS + 6 * CHUNKS + q
                send(pu.at[r, place, b, chunk(q)], uq.at[r, chunk(q)], index, far_dev)

    def scatter_users_total(r):
        scatter_users_sum(r, 1)
        total = pu[r, slot, b]
        if r:
            for q in range(CHUNKS):
                arrive(uq.at[r, chunk(q)], r * PER_ROUND + U_RS + 6 * CHUNKS + q, far_dev)
            total = total + uq[r]
        return total

    def gather_items_start(r, items):
        base = r * PER_ROUND
        if r:
            ib[r, zhi, y, core, c] = items
        mine = ib.at[r, zhi, y, core, c]
        for k in FAR_FIRST:
            send(mine, mine, base + Z_AG + k - 1, z_dev(k)[0])
        pass_on(r, 0)

    def pass_on(r, k):
        base = r * PER_ROUND
        hi, lo = along_z(k)
        piece = ib.at[r, hi, y, core, lo]
        for d in (2, 1, 3):
            send(piece, piece, base + Y_AG + (d - 1) * 8 + k, y_dev(d))
        send(piece, piece, base + C_AG + k, sib)

    def gather_items_z(r, steps):
        base = r * PER_ROUND
        for k in steps:
            hi, lo = along_z(k)
            arrive(ib.at[r, hi, y, core, lo], base + Z_AG + (8 - k) - 1, z_dev(k)[0])
            pass_on(r, k)

    def gather_items_y(r, steps):
        base = r * PER_ROUND
        for k in steps:
            hi, lo = along_z(k)
            for d in (1, 3, 2):
                piece = ib.at[r, hi, (y + d) % 4, core, lo]
                arrive(piece, base + Y_AG + (3 - d) * 8 + k, y_dev(d))
                send(piece, piece, base + C_AG + d * 8 + k, sib)

    def gather_items_end(r):
        base = r * PER_ROUND
        for k in (0,) + NEAR_FIRST:
            hi, lo = along_z(k)
            for d in range(4):
                piece = ib.at[r, hi, (y + d) % 4, 1 - core, lo]
                arrive(piece, base + C_AG + d * 8 + k, sib)

    def scatter_items_core(r):
        base = r * PER_ROUND
        for d in (2, 1, 3, 0):
            other = (y + d) % 4
            send(pi.at[r, :, other, 1 - core], rc.at[r, :, other], base + C_RS + d, sib)

    def scatter_items_y(r):
        base = r * PER_ROUND
        for d in (2, 1, 3, 0):
            other = (y + d) % 4
            arrive(rc.at[r, :, other], base + C_RS + d, sib)
            sums = pi[r, :, other, core] + rc[r, :, other]
            hb[r, other] = sums.reshape(8, 16, 256)
        for k in FAR_FIRST + (0,):
            at = (z + k) % 8
            for d in (2, 1, 3):
                source = hb.at[r, (y + d) % 4, at]
                send(source, yb[d - 1].at[r, at], base + Y_RS + (d - 1) * 8 + k, y_dev(d))

    def scatter_items_z(r, steps):
        base = r * PER_ROUND
        for k in steps:
            at = (z + k) % 8
            total = hb[r, y, at]
            for d in range(1, 4):
                arrive(yb[d - 1].at[r, at], base + Y_RS + (d - 1) * 8 + k, y_dev(d))
                total = total + yb[d - 1][r, at]
            zs[r, at] = total
            if k:
                send(zs.at[r, at], zb.at[r, k - 1], base + Z_RS + k - 1, z_dev(k)[0])

    def scatter_items_total(r):
        base = r * PER_ROUND
        total = zs[r, z]
        for k in NEAR_FIRST:
            arrive(zb.at[r, k - 1], base + Z_RS + k - 1, z_dev(8 - k)[0])
            total = total + zb[r, k - 1]
        return total

    def store_items(r, m, value):
        first = 2 * m % 4
        pi[r, m // 2, first : first + 2] = value.reshape(2, 2, 64, 256)

    def scatter(r):
        if r:
            scatter_users_forward(r, 0)
        scatter_items_y(r)
        scatter_users_forward(r, 1)
        if r == 0:
            to_scalars.wait()
            place_tiles(0)
        scatter_items_z(r, FAR_FIRST[:3])
        if r:
            scatter_users_sum(r, 0)
        scatter_items_z(r, FAR_FIRST[3:] + (0,))
        if r == 0:
            send_tiles(EARLY, EARLY + 1)
        users = scatter_users_total(r)
        if r:
            users = gu[...] + users
        else:
            gu[...] = users
        if r < LAYERS:
            gather_users_start(r + 1, users)
        items = scatter_items_total(r)
        if r:
            items = gi[...] + items
        else:
            gi[...] = items
        return users, items

    def send_tiles(first, last):
        for n in range(first, last):
            h = n // 3
            start = (2 * h + 1 - c % 2) * GROUP + n % 3 * PIECE
            send(
                tiles_ref.at[pl.ds(start, PIECE)],
                tbuf[h].at[1, pl.ds(n % 3 * PIECE, PIECE)],
                TILES + n,
                pair_dev,
            )

    def place_tiles(h):
        own_tiles[h].wait()
        for n in range(3 * h, 3 * h + 3):
            arrive(tbuf[h].at[1, pl.ds(n % 3 * PIECE, PIECE)], TILES + n, pair_dev)

        def place(row, carry):
            at_row = pl.ds(pl.multiple_of(h * 512 + row * 128, 128), 128)
            for col in range(8):
                at_col = slice(col * 128, (col + 1) * 128)
                spot = (2 * h + c % 2) * PLACES + row * 8 + col
                tile = tbuf[h][0, sints[0, 0, spot]] + tbuf[h][1, sints[1, 0, spot]]
                ah[at_row, at_col], al[at_row, at_col] = split2(tile)
                ath[at_col, at_row], atl[at_col, at_row] = split2(tile.T)
            return carry

        lax.fori_loop(0, 4, place, 0)

    to_scalars = pltpu.make_async_copy(gsource, sints, lsem.at[2])

    def loss_gradient():
        for k in range(1, 4):
            dev, other = hot_dev(k)
            send(gints.at[0], gints.at[k], INTS + k - 1, dev)
        send(gsource.at[0], gsource.at[1], SOURCE, pair_dev)
        gather_items_start(0, None)
        gather_users_start(0, None)
        send_tiles(0, EARLY)
        gather_items_z(0, NEAR_FIRST[:2])
        gather_users_forward(0)
        for k in range(1, 4):
            arrive(gints.at[k], INTS + k - 1, hot_dev(4 - k)[0])
        arrive(gsource.at[1], SOURCE, pair_dev)
        to_scalars.start()
        gather_items_z(0, NEAR_FIRST[2:])
        for k in range(1, 4):
            select_users(k)
        gather_items_y(0, (0,) + NEAR_FIRST[:4])
        for k in range(1, 4):
            select_items(k)
        gather_items_y(0, NEAR_FIRST[4:])
        gather_users_end(0)
        ut[0], ut[1], ut[2] = split3(ub[0, slot].reshape(512, 256))
        for h in range(4):
            span = slice(h * 256, (h + 1) * 256)
            hot = uho[span]
            buy[span] = dot(hot, ut[0]) + dot(hot, ut[1]) + dot(hot, ut[2])
        gather_items_end(0)
        dt[0], dt[1], dt[2] = split3(ib[0].reshape(1024, 256))
        for h in range(4):
            span = slice(h * 256, (h + 1) * 256)
            buyer, signed = buy[span], dho[span]
            differ = dot(signed, dt[0]) + dot(signed, dt[1]) + dot(signed, dt[2])
            margin = jnp.sum(buyer * differ, axis=1, keepdims=True)
            small = jnp.exp(-jnp.abs(margin))
            coef = -jnp.where(margin >= 0, small, 1.0) / (1.0 + small)
            wu[0, span], wu[1, span] = split2(coef * buyer)
            wd[0, span], wd[1, span] = split2(coef * differ)
        for m in range(4):
            left = ohd[m * 256 : (m + 1) * 256, :]
            store_items(0, m, dot(left, wu[0]) + dot(left, wu[1]))
        scatter_items_core(0)
        sums = dot(ohu[...], wd[0]) + dot(ohu[...], wd[1])
        pu[0, slot] = sums.reshape(4, 128, 256)
        scatter_users_start(0, 1)
        return scatter(0)

    def layer(r, items):
        gather_items_start(r, items)
        gather_users_over_z(r)
        if r == 1:
            send_tiles(EARLY + 1, PIECES)
        gather_items_z(r, NEAR_FIRST[:2])
        gather_users_forward(r)
        gather_items_z(r, NEAR_FIRST[2:6])
        gather_users_far(r, (0, 1))
        gather_items_z(r, NEAR_FIRST[6:])
        gather_items_y(r, (0,) + NEAR_FIRST[:4])
        gather_users_far(r, (2, 3))
        gather_items_y(r, NEAR_FIRST[4:])
        gather_items_end(r)
        if r == 1:
            place_tiles(1)
        xh, xl = split2(ib[r].reshape(1024, 256))
        for own in range(2):
            place = place_of(own)
            rows = pl.ds(pl.multiple_of(place * 512, 512), 512)
            sums = dot(ah[rows], xh) + dot(ah[rows], xl) + dot(al[rows], xh)
            pu[r, place] = sums.reshape(4, 128, 256)
            scatter_users_start(r, own)
        gather_users_end(r)
        uh, ul = split2(ub[r].reshape(1024, 256))
        for m in range(4):
            rows = slice(m * 256, (m + 1) * 256)
            store_items(r, m, dot(ath[rows], uh) + dot(ath[rows], ul) + dot(atl[rows], uh))
        scatter_items_core(r)
        return scatter(r)

    def rounds():
        users, items = loss_gradient()
        for r in range(1, ROUNDS):
            users, items = layer(r, items)
        return users, items

    users, items = rounds()
    uo_ref[...] = users / (LAYERS + 1.0)
    io_ref[...] = items / (LAYERS + 1.0)
    for copy in started:
        copy.wait_send()


def body(user_final, item_final, tiles, tile_rows, tile_cols, tile_count, triplets):
    slot = jnp.arange(4 * GROUP, dtype=jnp.int32)
    spot = slot // GROUP * PLACES + tile_rows // 4 * 8 + tile_cols
    spot = jnp.where(slot < tile_count[0], spot, -1)
    vmem = pl.BlockSpec(memory_space=pltpu.VMEM)
    smem = pl.BlockSpec(memory_space=pltpu.SMEM)
    hbm = pl.BlockSpec(memory_space=pltpu.HBM)
    return pl.pallas_call(
        kernel,
        out_shape=(
            jax.ShapeDtypeStruct((128, 256), F32),
            jax.ShapeDtypeStruct((16, 256), F32),
        ),
        in_specs=[vmem, smem, hbm, hbm, hbm],
        out_specs=(vmem, vmem),
        scratch_shapes=[
            pltpu.VMEM((4, 8, 256), jnp.int32),
            pltpu.VMEM((2, 1, 128), jnp.int32),
            pltpu.SMEM((2, 1, 128), jnp.int32),
            pltpu.VMEM((2, GROUP + 1, 128, 128), F32),
            pltpu.VMEM((2, GROUP + 1, 128, 128), F32),
            pltpu.VMEM((1024, 1024), BF16),
            pltpu.VMEM((1024, 1024), BF16),
            pltpu.VMEM((1024, 1024), BF16),
            pltpu.VMEM((1024, 1024), BF16),
            pltpu.VMEM((512, 1024), BF16),
            pltpu.VMEM((1024, 1024), BF16),
            pltpu.VMEM((1024, 512), BF16),
            pltpu.VMEM((1024, 1024), BF16),
            pltpu.VMEM((1024, 256), F32),
            pltpu.VMEM((3, 512, 256), BF16),
            pltpu.VMEM((3, 1024, 256), BF16),
            pltpu.VMEM((2, 1024, 256), BF16),
            pltpu.VMEM((2, 1024, 256), BF16),
            pltpu.VMEM((ROUNDS, 2, 4, 128, 256), F32),
            pltpu.VMEM((ROUNDS, 2, 4, 2, 4, 16, 256), F32),
            pltpu.VMEM((ROUNDS, 2, 4, 128, 256), F32),
            pltpu.VMEM((ROUNDS, 2, 4, 2, 64, 256), F32),
            pltpu.VMEM((ROUNDS, 2, 128, 256), F32),
            pltpu.VMEM((ROUNDS, 2, 128, 256), F32),
            pltpu.VMEM((ROUNDS, 2, 128, 256), F32),
            pltpu.VMEM((ROUNDS, 128, 256), F32),
            pltpu.VMEM((ROUNDS, 2, 4, 64, 256), F32),
            pltpu.VMEM((ROUNDS, 4, 8, 16, 256), F32),
            pltpu.VMEM((ROUNDS, 8, 16, 256), F32),
            pltpu.VMEM((ROUNDS, 8, 16, 256), F32),
            pltpu.VMEM((ROUNDS, 8, 16, 256), F32),
            pltpu.VMEM((ROUNDS, 8, 16, 256), F32),
            pltpu.VMEM((ROUNDS, 7, 16, 256), F32),
            pltpu.VMEM((128, 256), F32),
            pltpu.VMEM((16, 256), F32),
            pltpu.SemaphoreType.DMA((COPIES,)),
            pltpu.SemaphoreType.DMA((COPIES,)),
            pltpu.SemaphoreType.DMA((6,)),
        ],
        compiler_params=pltpu.CompilerParams(
            collective_id=0, has_side_effects=True, vmem_limit_bytes=52 * 1024 * 1024
        ),
        name="propagate",
    )(triplets.T, spot, user_final, item_final, tiles)


def solution(mesh):
    placed = (
        P(("user", "item", "hot"), None),
        P(("user", "item", "hot"), None),
        P(("user", "item", "hot"), None, None),
        P(("user", "item", "hot")),
        P(("user", "item", "hot")),
        P(("user", "item", "hot")),
        P(("user", "item", "hot"), None),
    )
    return jax.shard_map(
        body,
        mesh=mesh,
        in_specs=placed,
        out_specs=(P(("user", "item", "hot"), None), P(("user", "item", "hot"), None)),
        check_vma=False,
    )
```

```python
import jax
import jax.numpy as jnp
from jax import lax
from jax.experimental import pallas as pl
from jax.experimental.pallas import tpu as pltpu
from jax.sharding import PartitionSpec as P

MESH = pl.DeviceIdType.MESH
F32 = jnp.float32
BF16 = jnp.bfloat16
LAYERS = 2


ROUNDS = LAYERS + 1
GROUP = 12
PLACES = 32

CHUNKS = 4
CHUNK = 32
PIECES = 12
PIECE = 2
EARLY = 8
MIDDLE = 10

U_AG = 0
Z_AG = U_AG + 7 * CHUNKS
Y_AG = Z_AG + 7
C_AG = Y_AG + 24
C_RS = C_AG + 32
Y_RS = C_RS + 4
Z_RS = Y_RS + 24
U_RS = Z_RS + 7
PER_ROUND = U_RS + 7 * CHUNKS
INTS = PER_ROUND * ROUNDS
SOURCE = INTS + 3
TILES = SOURCE + 1
COPIES = TILES + PIECES
NEAR_FIRST = (1, 7, 2, 6, 3, 5, 4)
FAR_FIRST = (4, 5, 3, 6, 2, 7, 1)


def split2(x):
    hi = x.astype(BF16)
    return hi, (x - hi.astype(F32)).astype(BF16)


def split3(x):
    hi = x.astype(BF16)
    rest = x - hi.astype(F32)
    mid = rest.astype(BF16)
    return hi, mid, (rest - mid.astype(F32)).astype(BF16)


def dot(a, b):
    return jnp.dot(a, b, preferred_element_type=F32)


def kernel(
    trip_ref,
    spot_ref,
    uf_ref,
    if_ref,
    tiles_ref,
    uo_ref,
    io_ref,
    gints,
    gsource,
    sints,
    tbuf0,
    tbuf1,
    ah,
    al,
    ath,
    atl,
    ohu,
    ohd,
    uho,
    dho,
    buy,
    ut,
    dt,
    wd,
    wu,
    ub,
    ib,
    pu,
    pi,
    um,
    ua,
    uz,
    uq,
    rc,
    hb,
    ym,
    ya,
    yz,
    zs,
    zb,
    gu,
    gi,
    ssem,
    rsem,
    lsem,
):
    a = lax.axis_index("user")
    b = lax.axis_index("item")
    c = lax.axis_index("hot")
    core = a % 2
    y = (a // 2) % 4
    zhi = a // 8
    z = zhi * 4 + c

    def user_index(zhi_, y_, core_):
        return (zhi_ * 4 + y_) * 2 + core_

    def ring(v):
        even = v + 1 - 2 * (v % 2)
        odd = 3 - v
        first = (1 - core) * even + core * odd
        second = (1 - core) * odd + core * even
        return first, second, (v + 2) % 4

    x1, x2, xo = ring(b)
    xa_dev = (a, x1, c)
    xb_dev = (a, x2, c)
    xo_dev = (a, xo, c)
    tbuf = (tbuf0, tbuf1)
    yb = (ym, ya, yz)
    slot = c // 2
    pair = c + 1 - 2 * (c % 2)
    pair_dev = (a, b, pair)
    far_dev = (a, b, (c + 2) % 4)
    sib = (user_index(zhi, y, 1 - core), b, c)

    def z_dev(k):
        other = (z + k) % 8
        return (user_index(other // 4, y, core), b, other % 4), other // 4, other % 4

    def y_dev(k):
        other = (y + k) % 4
        return (user_index(zhi, other, core), b, c)

    def hot_dev(k):
        other = (c + k) % 4
        return (a, b, other), other

    started = []

    def send(src, dst, index, dev):
        copy = pltpu.make_async_remote_copy(
            src_ref=src,
            dst_ref=dst,
            send_sem=ssem.at[index],
            recv_sem=rsem.at[index],
            device_id=dev,
            device_id_type=MESH,
        )
        copy.start()
        started.append(copy)

    def arrive(dst, index, dev):
        pltpu.make_async_remote_copy(
            src_ref=dst,
            dst_ref=dst,
            send_sem=ssem.at[index],
            recv_sem=rsem.at[index],
            device_id=dev,
            device_id_type=MESH,
        ).wait_recv()

    barrier = pltpu.get_barrier_semaphore()
    peers = [xa_dev, xb_dev, xo_dev, sib]
    peers += [y_dev(k) for k in range(1, 4)] + [z_dev(k)[0] for k in range(1, 8)]
    for dev in peers:
        pl.semaphore_signal(barrier, inc=1, device_id=dev, device_id_type=MESH)
    own_tiles = [
        pltpu.make_async_copy(
            tiles_ref.at[pl.ds((2 * h + c % 2) * GROUP, GROUP)],
            tbuf[h].at[0, pl.ds(0, GROUP)],
            lsem.at[h],
        )
        for h in range(2)
    ]
    for copy in own_tiles:
        copy.start()
    shares = [
        pltpu.make_async_copy(uf_ref, ub.at[0, slot, b], lsem.at[4]),
        pltpu.make_async_copy(if_ref, ib.at[0, zhi, y, core, c], lsem.at[5]),
    ]
    for copy in shares:
        copy.start()
    for h in range(2):
        tbuf[h][0, GROUP] = jnp.zeros((128, 128), F32)
        tbuf[h][1, GROUP] = jnp.zeros((128, 128), F32)
    for copy in shares:
        copy.wait()
    lanes = lax.broadcasted_iota(jnp.int32, (1, 128), 1)
    source = jnp.full((1, 128), GROUP, jnp.int32)
    for n in range(4 * GROUP):
        source = jnp.where(lanes == spot_ref[n], n % GROUP, source)
    gsource[0] = source
    buyers = trip_ref[0:1] % 2048
    gints[0, 0:1] = buyers // 512 * 128 + buyers % 128
    gints[0, 1:2] = buyers // 128 % 4
    gints[0, 2:3] = trip_ref[1:2] // 256 * 64 + trip_ref[1:2] % 64
    gints[0, 3:4] = trip_ref[2:3] // 256 * 64 + trip_ref[2:3] % 64
    gints[0, 4:8] = jnp.zeros((4, 256), jnp.int32)
    count_up = lax.broadcasted_iota(jnp.int32, (256, 256), 0).astype(F32).astype(BF16)

    def one_hot(index, m):
        inside = jnp.where(index // 256 == m, index % 256, -1).astype(F32)
        inside = jnp.broadcast_to(inside, (256, 256)).astype(BF16)
        return jnp.where(count_up == inside, jnp.ones((), BF16), jnp.zeros((), BF16))

    count_right = lax.broadcasted_iota(jnp.int32, (256, 256), 1).astype(F32).astype(BF16)

    def one_hot_rows(index, m):
        inside = jnp.where(index // 256 == m, index % 256, -1).astype(F32)
        inside = jnp.broadcast_to(inside, (256, 256)).astype(BF16)
        return jnp.where(count_right == inside, jnp.ones((), BF16), jnp.zeros((), BF16))

    def select_users(k):
        buyers = jnp.where(gints[k, 1:2, :] == c, gints[k, 0:1, :], -1)
        columns = gints[k].T
        column = jnp.where(columns[:, 1:2] == c, columns[:, 0:1], -1)
        for m in range(2):
            block = slice(m * 256, (m + 1) * 256)
            span = slice(k * 256, (k + 1) * 256)
            ohu[block, span] = one_hot(buyers, m)
            uho[span, block] = one_hot_rows(column, m)

    def select_items(k):
        columns = gints[k].T
        for m in range(4):
            block = slice(m * 256, (m + 1) * 256)
            span = slice(k * 256, (k + 1) * 256)
            ohd[block, span] = one_hot(gints[k, 2:3, :], m) - one_hot(gints[k, 3:4, :], m)
            chosen = one_hot_rows(columns[:, 2:3], m)
            dho[span, block] = chosen - one_hot_rows(columns[:, 3:4], m)

    select_users(0)
    select_items(0)
    pl.semaphore_wait(barrier, len(peers))

    def chunk(q):
        return pl.ds(q * CHUNK, CHUNK)

    def place_of(own):
        return slot if own else 1 - slot

    def along_z(k):
        other = (z + k) % 8
        return other // 4, other % 4

    def gather_users_start(r, users):
        base = r * PER_ROUND + U_AG
        if r:
            ub[r, slot, b] = users
        for q in range(CHUNKS):
            mine = ub.at[r, slot, b, chunk(q)]
            send(mine, mine, base + q, xa_dev)
            send(mine, mine, base + CHUNKS + q, xb_dev)

    def gather_users_over_z(r):
        for q in range(CHUNKS):
            mine = ub.at[r, slot, b, chunk(q)]
            send(mine, mine, r * PER_ROUND + U_AG + 6 * CHUNKS + q, far_dev)

    def gather_users_far(r, chunks):
        base = r * PER_ROUND + U_AG
        for q in chunks:
            other = ub.at[r, 1 - slot, b, chunk(q)]
            arrive(other, base + 6 * CHUNKS + q, far_dev)
            send(other, other, base + 5 * CHUNKS + q, xo_dev)
            send(other, other, base + 3 * CHUNKS + q, xa_dev)
            send(other, other, base + 4 * CHUNKS + q, xb_dev)

    def gather_users_forward(r):
        base = r * PER_ROUND + U_AG
        for q in range(CHUNKS):
            block = ub.at[r, slot, x1, chunk(q)]
            arrive(block, base + q, xa_dev)
            send(block, block, base + 2 * CHUNKS + q, xb_dev)

    def gather_users_own(r):
        base = r * PER_ROUND + U_AG
        for q in range(CHUNKS):
            arrive(ub.at[r, slot, x2, chunk(q)], base + CHUNKS + q, xb_dev)
        for q in range(CHUNKS):
            arrive(ub.at[r, slot, xo, chunk(q)], base + 2 * CHUNKS + q, xb_dev)

    def gather_users_end(r):
        base = r * PER_ROUND + U_AG + 3 * CHUNKS
        for q in range(CHUNKS):
            arrive(ub.at[r, 1 - slot, x1, chunk(q)], base + q, xa_dev)
            arrive(ub.at[r, 1 - slot, x2, chunk(q)], base + CHUNKS + q, xb_dev)
            arrive(ub.at[r, 1 - slot, xo, chunk(q)], base + 2 * CHUNKS + q, xo_dev)

    def scatter_users_start(r, own):
        base = r * PER_ROUND + U_RS + 3 * CHUNKS * own
        place = place_of(own)
        for q in range(CHUNKS):
            send(pu.at[r, place, xo, chunk(q)], um.at[r, own, chunk(q)], base + q, xb_dev)
        for q in range(CHUNKS):
            send(pu.at[r, place, x2, chunk(q)], uz.at[r, own, chunk(q)], base + CHUNKS + q, xb_dev)

    def scatter_users_forward(r, own):
        base = r * PER_ROUND + U_RS + 3 * CHUNKS * own
        place = place_of(own)
        for q in range(CHUNKS):
            arrive(um.at[r, own, chunk(q)], base + q, xb_dev)
            pu[r, place, x1, chunk(q)] = pu[r, place, x1, chunk(q)] + um[r, own, chunk(q)]
            sums = pu.at[r, place, x1, chunk(q)]
            send(sums, ua.at[r, own, chunk(q)], base + 2 * CHUNKS + q, xa_dev)

    def scatter_users_sum(r, own):
        base = r * PER_ROUND + U_RS + 3 * CHUNKS * own
        place = place_of(own)
        for q in range(CHUNKS):
            arrive(uz.at[r, own, chunk(q)], base + CHUNKS + q, xb_dev)
            arrive(ua.at[r, own, chunk(q)], base + 2 * CHUNKS + q, xa_dev)
            sums = pu[r, place, b, chunk(q)] + uz[r, own, chunk(q)] + ua[r, own, chunk(q)]
            pu[r, place, b, chunk(q)] = sums
            if not own:
                index = r * PER_ROUND + U_RS + 6 * CHUNKS + q
                send(pu.at[r, place, b, chunk(q)], uq.at[r, chunk(q)], index, far_dev)

    def scatter_users_total(r):
        scatter_users_sum(r, 1)
        total = pu[r, slot, b]
        if r:
            for q in range(CHUNKS):
                arrive(uq.at[r, chunk(q)], r * PER_ROUND + U_RS + 6 * CHUNKS + q, far_dev)
            total = total + uq[r]
        return total

    def gather_items_start(r, items):
        base = r * PER_ROUND
        if r:
            ib[r, zhi, y, core, c] = items
        mine = ib.at[r, zhi, y, core, c]
        for k in FAR_FIRST:
            send(mine, mine, base + Z_AG + k - 1, z_dev(k)[0])
        pass_on(r, 0)

    def pass_on(r, k):
        base = r * PER_ROUND
        hi, lo = along_z(k)
        piece = ib.at[r, hi, y, core, lo]
        for d in (2, 1, 3):
            send(piece, piece, base + Y_AG + (d - 1) * 8 + k, y_dev(d))
        send(piece, piece, base + C_AG + k, sib)

    def gather_items_z(r, steps):
        base = r * PER_ROUND
        for k in steps:
            hi, lo = along_z(k)
            arrive(ib.at[r, hi, y, core, lo], base + Z_AG + (8 - k) - 1, z_dev(k)[0])
            pass_on(r, k)

    def gather_items_y(r, steps):
        base = r * PER_ROUND
        for k in steps:
            hi, lo = along_z(k)
            for d in (1, 3, 2):
                piece = ib.at[r, hi, (y + d) % 4, core, lo]
                arrive(piece, base + Y_AG + (3 - d) * 8 + k, y_dev(d))
                send(piece, piece, base + C_AG + d * 8 + k, sib)

    def gather_items_end(r):
        base = r * PER_ROUND
        for k in (0,) + NEAR_FIRST:
            hi, lo = along_z(k)
            for d in range(4):
                piece = ib.at[r, hi, (y + d) % 4, 1 - core, lo]
                arrive(piece, base + C_AG + d * 8 + k, sib)

    def scatter_items_core(r):
        base = r * PER_ROUND
        for d in (2, 1, 3, 0):
            other = (y + d) % 4
            send(pi.at[r, :, other, 1 - core], rc.at[r, :, other], base + C_RS + d, sib)

    def scatter_items_y(r):
        base = r * PER_ROUND
        for d in (2, 1, 3, 0):
            other = (y + d) % 4
            arrive(rc.at[r, :, other], base + C_RS + d, sib)
            sums = pi[r, :, other, core] + rc[r, :, other]
            hb[r, other] = sums.reshape(8, 16, 256)
        for k in FAR_FIRST + (0,):
            at = (z + k) % 8
            for d in (2, 1, 3):
                source = hb.at[r, (y + d) % 4, at]
                send(source, yb[d - 1].at[r, at], base + Y_RS + (d - 1) * 8 + k, y_dev(d))

    def scatter_items_z(r, steps):
        base = r * PER_ROUND
        for k in steps:
            at = (z + k) % 8
            total = hb[r, y, at]
            for d in range(1, 4):
                arrive(yb[d - 1].at[r, at], base + Y_RS + (d - 1) * 8 + k, y_dev(d))
                total = total + yb[d - 1][r, at]
            zs[r, at] = total
            if k:
                send(zs.at[r, at], zb.at[r, k - 1], base + Z_RS + k - 1, z_dev(k)[0])

    def scatter_items_total(r):
        base = r * PER_ROUND
        total = zs[r, z]
        for k in NEAR_FIRST:
            arrive(zb.at[r, k - 1], base + Z_RS + k - 1, z_dev(8 - k)[0])
            total = total + zb[r, k - 1]
        return total

    def store_items(r, m, value):
        first = 2 * m % 4
        pi[r, m // 2, first : first + 2] = value.reshape(2, 2, 64, 256)

    def scatter(r):
        if r:
            scatter_users_forward(r, 0)
        scatter_items_y(r)
        scatter_users_forward(r, 1)
        if r == 0:
            to_scalars.wait()
            place_tiles(0)
        scatter_items_z(r, FAR_FIRST[:3])
        if r:
            scatter_users_sum(r, 0)
        scatter_items_z(r, FAR_FIRST[3:] + (0,))
        if r == 0:
            send_tiles(EARLY, MIDDLE)
        users = scatter_users_total(r)
        if r:
            users = gu[...] + users
        else:
            gu[...] = users
        if r < LAYERS:
            gather_users_start(r + 1, users)
        items = scatter_items_total(r)
        if r:
            items = gi[...] + items
        else:
            gi[...] = items
        return users, items

    def send_tiles(first, last):
        for n in range(first, last):
            h = n // 6
            start = (2 * h + 1 - c % 2) * GROUP + n % 6 * PIECE
            send(
                tiles_ref.at[pl.ds(start, PIECE)],
                tbuf[h].at[1, pl.ds(n % 6 * PIECE, PIECE)],
                TILES + n,
                pair_dev,
            )

    def place_tiles(h):
        own_tiles[h].wait()
        for n in range(6 * h, 6 * h + 6):
            arrive(tbuf[h].at[1, pl.ds(n % 6 * PIECE, PIECE)], TILES + n, pair_dev)

        def place(row, carry):
            at_row = pl.ds(pl.multiple_of(h * 512 + row * 128, 128), 128)
            for col in range(8):
                at_col = slice(col * 128, (col + 1) * 128)
                spot = (2 * h + c % 2) * PLACES + row * 8 + col
                tile = tbuf[h][0, sints[0, 0, spot]] + tbuf[h][1, sints[1, 0, spot]]
                ah[at_row, at_col], al[at_row, at_col] = split2(tile)
                ath[at_col, at_row], atl[at_col, at_row] = split2(tile.T)
            return carry

        lax.fori_loop(0, 4, place, 0)

    to_scalars = pltpu.make_async_copy(gsource, sints, lsem.at[2])

    def loss_gradient():
        for k in range(1, 4):
            dev, other = hot_dev(k)
            send(gints.at[0], gints.at[k], INTS + k - 1, dev)
        send(gsource.at[0], gsource.at[1], SOURCE, pair_dev)
        gather_items_start(0, None)
        gather_users_start(0, None)
        send_tiles(0, EARLY)
        gather_items_z(0, NEAR_FIRST[:2])
        gather_users_forward(0)
        for k in range(1, 4):
            arrive(gints.at[k], INTS + k - 1, hot_dev(4 - k)[0])
        arrive(gsource.at[1], SOURCE, pair_dev)
        to_scalars.start()
        gather_items_z(0, NEAR_FIRST[2:])
        for k in range(1, 4):
            select_users(k)
        gather_items_y(0, (0,) + NEAR_FIRST[:4])
        for k in range(1, 4):
            select_items(k)
        gather_items_y(0, NEAR_FIRST[4:])
        gather_users_own(0)
        ut[0], ut[1], ut[2] = split3(ub[0, slot].reshape(512, 256))
        for h in range(4):
            span = slice(h * 256, (h + 1) * 256)
            hot = uho[span]
            buy[span] = dot(hot, ut[0]) + dot(hot, ut[1]) + dot(hot, ut[2])
        gather_items_end(0)
        dt[0], dt[1], dt[2] = split3(ib[0].reshape(1024, 256))
        for h in range(4):
            span = slice(h * 256, (h + 1) * 256)
            buyer, signed = buy[span], dho[span]
            differ = dot(signed, dt[0]) + dot(signed, dt[1]) + dot(signed, dt[2])
            margin = jnp.sum(buyer * differ, axis=1, keepdims=True)
            small = jnp.exp(-jnp.abs(margin))
            coef = -jnp.where(margin >= 0, small, 1.0) / (1.0 + small)
            wu[0, span], wu[1, span] = split2(coef * buyer)
            wd[0, span], wd[1, span] = split2(coef * differ)
        for m in range(4):
            left = ohd[m * 256 : (m + 1) * 256, :]
            store_items(0, m, dot(left, wu[0]) + dot(left, wu[1]))
        scatter_items_core(0)
        sums = dot(ohu[...], wd[0]) + dot(ohu[...], wd[1])
        pu[0, slot] = sums.reshape(4, 128, 256)
        scatter_users_start(0, 1)
        return scatter(0)

    def add_items(r, place, more):
        uh, ul = split2(ub[r, place].reshape(512, 256))
        users = pl.ds(pl.multiple_of(place * 512, 512), 512)
        for m in range(4):
            rows = slice(m * 256, (m + 1) * 256)
            high, low = ath[rows, users], atl[rows, users]
            sums = dot(high, uh) + dot(high, ul) + dot(low, uh)
            first = 2 * m % 4
            sums = sums.reshape(2, 2, 64, 256)
            if more:
                sums = sums + pi[r, m // 2, first : first + 2]
            pi[r, m // 2, first : first + 2] = sums

    def layer(r, items):
        gather_items_start(r, items)
        gather_users_over_z(r)
        if r == 1:
            send_tiles(MIDDLE, PIECES)
        gather_items_z(r, NEAR_FIRST[:2])
        gather_users_forward(r)
        gather_items_z(r, NEAR_FIRST[2:6])
        gather_users_far(r, (0, 1))
        gather_items_z(r, NEAR_FIRST[6:])
        gather_items_y(r, (0,) + NEAR_FIRST[:4])
        gather_users_far(r, (2, 3))
        gather_items_y(r, NEAR_FIRST[4:])
        if r == 1:
            place_tiles(1)
        gather_users_own(r)
        add_items(r, slot, False)
        gather_items_end(r)
        xh, xl = split2(ib[r].reshape(1024, 256))
        for own in range(2):
            place = place_of(own)
            rows = pl.ds(pl.multiple_of(place * 512, 512), 512)
            sums = dot(ah[rows], xh) + dot(ah[rows], xl) + dot(al[rows], xh)
            pu[r, place] = sums.reshape(4, 128, 256)
            scatter_users_start(r, own)
        gather_users_end(r)
        add_items(r, 1 - slot, True)
        scatter_items_core(r)
        return scatter(r)

    def rounds():
        users, items = loss_gradient()
        for r in range(1, ROUNDS):
            users, items = layer(r, items)
        return users, items

    users, items = rounds()
    uo_ref[...] = users / (LAYERS + 1.0)
    io_ref[...] = items / (LAYERS + 1.0)
    for copy in started:
        copy.wait_send()


def body(user_final, item_final, tiles, tile_rows, tile_cols, tile_count, triplets):
    slot = jnp.arange(4 * GROUP, dtype=jnp.int32)
    spot = slot // GROUP * PLACES + tile_rows // 4 * 8 + tile_cols
    spot = jnp.where(slot < tile_count[0], spot, -1)
    vmem = pl.BlockSpec(memory_space=pltpu.VMEM)
    smem = pl.BlockSpec(memory_space=pltpu.SMEM)
    hbm = pl.BlockSpec(memory_space=pltpu.HBM)
    return pl.pallas_call(
        kernel,
        out_shape=(
            jax.ShapeDtypeStruct((128, 256), F32),
            jax.ShapeDtypeStruct((16, 256), F32),
        ),
        in_specs=[vmem, smem, hbm, hbm, hbm],
        out_specs=(vmem, vmem),
        scratch_shapes=[
            pltpu.VMEM((4, 8, 256), jnp.int32),
            pltpu.VMEM((2, 1, 128), jnp.int32),
            pltpu.SMEM((2, 1, 128), jnp.int32),
            pltpu.VMEM((2, GROUP + 1, 128, 128), F32),
            pltpu.VMEM((2, GROUP + 1, 128, 128), F32),
            pltpu.VMEM((1024, 1024), BF16),
            pltpu.VMEM((1024, 1024), BF16),
            pltpu.VMEM((1024, 1024), BF16),
            pltpu.VMEM((1024, 1024), BF16),
            pltpu.VMEM((512, 1024), BF16),
            pltpu.VMEM((1024, 1024), BF16),
            pltpu.VMEM((1024, 512), BF16),
            pltpu.VMEM((1024, 1024), BF16),
            pltpu.VMEM((1024, 256), F32),
            pltpu.VMEM((3, 512, 256), BF16),
            pltpu.VMEM((3, 1024, 256), BF16),
            pltpu.VMEM((2, 1024, 256), BF16),
            pltpu.VMEM((2, 1024, 256), BF16),
            pltpu.VMEM((ROUNDS, 2, 4, 128, 256), F32),
            pltpu.VMEM((ROUNDS, 2, 4, 2, 4, 16, 256), F32),
            pltpu.VMEM((ROUNDS, 2, 4, 128, 256), F32),
            pltpu.VMEM((ROUNDS, 2, 4, 2, 64, 256), F32),
            pltpu.VMEM((ROUNDS, 2, 128, 256), F32),
            pltpu.VMEM((ROUNDS, 2, 128, 256), F32),
            pltpu.VMEM((ROUNDS, 2, 128, 256), F32),
            pltpu.VMEM((ROUNDS, 128, 256), F32),
            pltpu.VMEM((ROUNDS, 2, 4, 64, 256), F32),
            pltpu.VMEM((ROUNDS, 4, 8, 16, 256), F32),
            pltpu.VMEM((ROUNDS, 8, 16, 256), F32),
            pltpu.VMEM((ROUNDS, 8, 16, 256), F32),
            pltpu.VMEM((ROUNDS, 8, 16, 256), F32),
            pltpu.VMEM((ROUNDS, 8, 16, 256), F32),
            pltpu.VMEM((ROUNDS, 7, 16, 256), F32),
            pltpu.VMEM((128, 256), F32),
            pltpu.VMEM((16, 256), F32),
            pltpu.SemaphoreType.DMA((COPIES,)),
            pltpu.SemaphoreType.DMA((COPIES,)),
            pltpu.SemaphoreType.DMA((6,)),
        ],
        compiler_params=pltpu.CompilerParams(
            collective_id=0, has_side_effects=True, vmem_limit_bytes=52 * 1024 * 1024
        ),
        name="propagate",
    )(triplets.T, spot, user_final, item_final, tiles)


def solution(mesh):
    placed = (
        P(("user", "item", "hot"), None),
        P(("user", "item", "hot"), None),
        P(("user", "item", "hot"), None, None),
        P(("user", "item", "hot")),
        P(("user", "item", "hot")),
        P(("user", "item", "hot")),
        P(("user", "item", "hot"), None),
    )
    return jax.shard_map(
        body,
        mesh=mesh,
        in_specs=placed,
        out_specs=(P(("user", "item", "hot"), None), P(("user", "item", "hot"), None)),
        check_vma=False,
    )
```

```python
import jax
import jax.numpy as jnp
from jax import lax
from jax.experimental import pallas as pl
from jax.experimental.pallas import tpu as pltpu
from jax.sharding import PartitionSpec as P

MESH = pl.DeviceIdType.MESH
F32 = jnp.float32
BF16 = jnp.bfloat16
LAYERS = 2


ROUNDS = LAYERS + 1
GROUP = 12
PLACES = 32

CHUNKS = 4
CHUNK = 32
PIECES = 12
PIECE = 2
EARLY = 8
MIDDLE = 10

U_AG = 0
Z_AG = U_AG + 7 * CHUNKS
Y_AG = Z_AG + 7
C_AG = Y_AG + 24
C_RS = C_AG + 32
Y_RS = C_RS + 4
Z_RS = Y_RS + 24
U_RS = Z_RS + 7
PER_ROUND = U_RS + 7 * CHUNKS
INTS = PER_ROUND * ROUNDS
SOURCE = INTS + 3
TILES = SOURCE + 1
COPIES = TILES + PIECES
NEAR_FIRST = (1, 7, 2, 6, 3, 5, 4)
FAR_FIRST = (4, 5, 3, 6, 2, 7, 1)


def split2(x):
    hi = x.astype(BF16)
    return hi, (x - hi.astype(F32)).astype(BF16)


def split3(x):
    hi = x.astype(BF16)
    rest = x - hi.astype(F32)
    mid = rest.astype(BF16)
    return hi, mid, (rest - mid.astype(F32)).astype(BF16)


def dot(a, b):
    return jnp.dot(a, b, preferred_element_type=F32)


def kernel(
    trip_ref,
    spot_ref,
    uf_ref,
    if_ref,
    tiles_ref,
    uo_ref,
    io_ref,
    gints,
    gsource,
    sints,
    tbuf0,
    tbuf1,
    ah,
    al,
    ath,
    atl,
    ohu,
    ohd,
    uho,
    dho,
    buy,
    ut,
    dt,
    wd,
    wu,
    ub,
    ib,
    pu,
    pi,
    um,
    ua,
    uz,
    uq,
    rc,
    hb,
    ym,
    ya,
    yz,
    zs,
    zb,
    gu,
    gi,
    ssem,
    rsem,
    lsem,
):
    a = lax.axis_index("user")
    b = lax.axis_index("item")
    c = lax.axis_index("hot")
    core = a % 2
    y = (a // 2) % 4
    zhi = a // 8
    z = zhi * 4 + c

    def user_index(zhi_, y_, core_):
        return (zhi_ * 4 + y_) * 2 + core_

    def ring(v):
        even = v + 1 - 2 * (v % 2)
        odd = 3 - v
        first = (1 - core) * even + core * odd
        second = (1 - core) * odd + core * even
        return first, second, (v + 2) % 4

    x1, x2, xo = ring(b)
    xa_dev = (a, x1, c)
    xb_dev = (a, x2, c)
    xo_dev = (a, xo, c)
    tbuf = (tbuf0, tbuf1)
    yb = (ym, ya, yz)
    slot = c // 2
    pair = c + 1 - 2 * (c % 2)
    pair_dev = (a, b, pair)
    far_dev = (a, b, (c + 2) % 4)
    sib = (user_index(zhi, y, 1 - core), b, c)

    def z_dev(k):
        other = (z + k) % 8
        return (user_index(other // 4, y, core), b, other % 4), other // 4, other % 4

    def y_dev(k):
        other = (y + k) % 4
        return (user_index(zhi, other, core), b, c)

    def hot_dev(k):
        other = (c + k) % 4
        return (a, b, other), other

    started = []

    def send(src, dst, index, dev):
        copy = pltpu.make_async_remote_copy(
            src_ref=src,
            dst_ref=dst,
            send_sem=ssem.at[index],
            recv_sem=rsem.at[index],
            device_id=dev,
            device_id_type=MESH,
        )
        copy.start()
        started.append(copy)

    def arrive(dst, index, dev):
        pltpu.make_async_remote_copy(
            src_ref=dst,
            dst_ref=dst,
            send_sem=ssem.at[index],
            recv_sem=rsem.at[index],
            device_id=dev,
            device_id_type=MESH,
        ).wait_recv()

    barrier = pltpu.get_barrier_semaphore()
    peers = [xa_dev, xb_dev, xo_dev, sib]
    peers += [y_dev(k) for k in range(1, 4)] + [z_dev(k)[0] for k in range(1, 8)]
    for dev in peers:
        pl.semaphore_signal(barrier, inc=1, device_id=dev, device_id_type=MESH)
    own_tiles = [
        pltpu.make_async_copy(
            tiles_ref.at[pl.ds((2 * h + c % 2) * GROUP, GROUP)],
            tbuf[h].at[0, pl.ds(0, GROUP)],
            lsem.at[h],
        )
        for h in range(2)
    ]
    for copy in own_tiles:
        copy.start()
    shares = [
        pltpu.make_async_copy(uf_ref, ub.at[0, slot, b], lsem.at[4]),
        pltpu.make_async_copy(if_ref, ib.at[0, zhi, y, core, c], lsem.at[5]),
    ]
    for copy in shares:
        copy.start()
    for h in range(2):
        tbuf[h][0, GROUP] = jnp.zeros((128, 128), F32)
        tbuf[h][1, GROUP] = jnp.zeros((128, 128), F32)
    for copy in shares:
        copy.wait()
    lanes = lax.broadcasted_iota(jnp.int32, (1, 128), 1)
    source = jnp.full((1, 128), GROUP, jnp.int32)
    for n in range(4 * GROUP):
        source = jnp.where(lanes == spot_ref[n], n % GROUP, source)
    gsource[0] = source
    buyers = trip_ref[0:1] % 2048
    gints[0, 0:1] = buyers // 512 * 128 + buyers % 128
    gints[0, 1:2] = buyers // 128 % 4
    gints[0, 2:3] = trip_ref[1:2] // 256 * 64 + trip_ref[1:2] % 64
    gints[0, 3:4] = trip_ref[2:3] // 256 * 64 + trip_ref[2:3] % 64
    gints[0, 4:8] = jnp.zeros((4, 256), jnp.int32)
    count_up = lax.broadcasted_iota(jnp.int32, (256, 256), 0).astype(F32).astype(BF16)

    def one_hot(index, m):
        inside = jnp.where(index // 256 == m, index % 256, -1).astype(F32)
        inside = jnp.broadcast_to(inside, (256, 256)).astype(BF16)
        return jnp.where(count_up == inside, jnp.ones((), BF16), jnp.zeros((), BF16))

    count_right = lax.broadcasted_iota(jnp.int32, (256, 256), 1).astype(F32).astype(BF16)

    def one_hot_rows(index, m):
        inside = jnp.where(index // 256 == m, index % 256, -1).astype(F32)
        inside = jnp.broadcast_to(inside, (256, 256)).astype(BF16)
        return jnp.where(count_right == inside, jnp.ones((), BF16), jnp.zeros((), BF16))

    def select_users(k):
        buyers = jnp.where(gints[k, 1:2, :] == c, gints[k, 0:1, :], -1)
        columns = gints[k].T
        column = jnp.where(columns[:, 1:2] == c, columns[:, 0:1], -1)
        for m in range(2):
            block = slice(m * 256, (m + 1) * 256)
            span = slice(k * 256, (k + 1) * 256)
            ohu[block, span] = one_hot(buyers, m)
            uho[span, block] = one_hot_rows(column, m)

    def select_items(k):
        columns = gints[k].T
        for m in range(4):
            block = slice(m * 256, (m + 1) * 256)
            span = slice(k * 256, (k + 1) * 256)
            ohd[block, span] = one_hot(gints[k, 2:3, :], m) - one_hot(gints[k, 3:4, :], m)
            chosen = one_hot_rows(columns[:, 2:3], m)
            dho[span, block] = chosen - one_hot_rows(columns[:, 3:4], m)

    select_users(0)
    select_items(0)
    pl.semaphore_wait(barrier, len(peers))

    def chunk(q):
        return pl.ds(q * CHUNK, CHUNK)

    def place_of(own):
        return slot if own else 1 - slot

    def along_z(k):
        other = (z + k) % 8
        return other // 4, other % 4

    def gather_users_start(r, users):
        base = r * PER_ROUND + U_AG
        if r:
            ub[r, slot, b] = users
        for q in range(CHUNKS):
            mine = ub.at[r, slot, b, chunk(q)]
            send(mine, mine, base + q, xa_dev)
            send(mine, mine, base + CHUNKS + q, xb_dev)

    def gather_users_over_z(r):
        for q in range(CHUNKS):
            mine = ub.at[r, slot, b, chunk(q)]
            send(mine, mine, r * PER_ROUND + U_AG + 6 * CHUNKS + q, far_dev)

    def gather_users_far(r, chunks):
        base = r * PER_ROUND + U_AG
        for q in chunks:
            other = ub.at[r, 1 - slot, b, chunk(q)]
            arrive(other, base + 6 * CHUNKS + q, far_dev)
            send(other, other, base + 5 * CHUNKS + q, xo_dev)
            send(other, other, base + 3 * CHUNKS + q, xa_dev)
            send(other, other, base + 4 * CHUNKS + q, xb_dev)

    def gather_users_forward(r):
        base = r * PER_ROUND + U_AG
        for q in range(CHUNKS):
            block = ub.at[r, slot, x1, chunk(q)]
            arrive(block, base + q, xa_dev)
            send(block, block, base + 2 * CHUNKS + q, xb_dev)

    def gather_users_end(r):
        base = r * PER_ROUND + U_AG
        for q in range(CHUNKS):
            arrive(ub.at[r, slot, x2, chunk(q)], base + CHUNKS + q, xb_dev)
        for q in range(CHUNKS):
            arrive(ub.at[r, slot, xo, chunk(q)], base + 2 * CHUNKS + q, xb_dev)
        if r:
            base = base + 3 * CHUNKS
            for q in range(CHUNKS):
                arrive(ub.at[r, 1 - slot, x1, chunk(q)], base + q, xa_dev)
                arrive(ub.at[r, 1 - slot, x2, chunk(q)], base + CHUNKS + q, xb_dev)
                arrive(ub.at[r, 1 - slot, xo, chunk(q)], base + 2 * CHUNKS + q, xo_dev)

    def scatter_users_start(r, own):
        base = r * PER_ROUND + U_RS + 3 * CHUNKS * own
        place = place_of(own)
        for q in range(CHUNKS):
            send(pu.at[r, place, xo, chunk(q)], um.at[r, own, chunk(q)], base + q, xb_dev)
        for q in range(CHUNKS):
            send(pu.at[r, place, x2, chunk(q)], uz.at[r, own, chunk(q)], base + CHUNKS + q, xb_dev)

    def scatter_users_forward(r, own):
        base = r * PER_ROUND + U_RS + 3 * CHUNKS * own
        place = place_of(own)
        for q in range(CHUNKS):
            arrive(um.at[r, own, chunk(q)], base + q, xb_dev)
            pu[r, place, x1, chunk(q)] = pu[r, place, x1, chunk(q)] + um[r, own, chunk(q)]
            sums = pu.at[r, place, x1, chunk(q)]
            send(sums, ua.at[r, own, chunk(q)], base + 2 * CHUNKS + q, xa_dev)

    def scatter_users_sum(r, own):
        base = r * PER_ROUND + U_RS + 3 * CHUNKS * own
        place = place_of(own)
        for q in range(CHUNKS):
            arrive(uz.at[r, own, chunk(q)], base + CHUNKS + q, xb_dev)
            arrive(ua.at[r, own, chunk(q)], base + 2 * CHUNKS + q, xa_dev)
            sums = pu[r, place, b, chunk(q)] + uz[r, own, chunk(q)] + ua[r, own, chunk(q)]
            pu[r, place, b, chunk(q)] = sums
            if not own:
                index = r * PER_ROUND + U_RS + 6 * CHUNKS + q
                send(pu.at[r, place, b, chunk(q)], uq.at[r, chunk(q)], index, far_dev)

    def scatter_users_total(r):
        scatter_users_sum(r, 1)
        total = pu[r, slot, b]
        if r:
            for q in range(CHUNKS):
                arrive(uq.at[r, chunk(q)], r * PER_ROUND + U_RS + 6 * CHUNKS + q, far_dev)
            total = total + uq[r]
        return total

    def gather_items_start(r, items):
        base = r * PER_ROUND
        if r:
            ib[r, zhi, y, core, c] = items
        mine = ib.at[r, zhi, y, core, c]
        for k in FAR_FIRST:
            send(mine, mine, base + Z_AG + k - 1, z_dev(k)[0])
        pass_on(r, 0)

    def pass_on(r, k):
        base = r * PER_ROUND
        hi, lo = along_z(k)
        piece = ib.at[r, hi, y, core, lo]
        for d in (2, 1, 3):
            send(piece, piece, base + Y_AG + (d - 1) * 8 + k, y_dev(d))
        send(piece, piece, base + C_AG + k, sib)

    def gather_items_z(r, steps):
        base = r * PER_ROUND
        for k in steps:
            hi, lo = along_z(k)
            arrive(ib.at[r, hi, y, core, lo], base + Z_AG + (8 - k) - 1, z_dev(k)[0])
            pass_on(r, k)

    def gather_items_y(r, steps):
        base = r * PER_ROUND
        for k in steps:
            hi, lo = along_z(k)
            for d in (1, 3, 2):
                piece = ib.at[r, hi, (y + d) % 4, core, lo]
                arrive(piece, base + Y_AG + (3 - d) * 8 + k, y_dev(d))
                send(piece, piece, base + C_AG + d * 8 + k, sib)

    def gather_items_end(r):
        base = r * PER_ROUND
        for k in (0,) + NEAR_FIRST:
            hi, lo = along_z(k)
            for d in range(4):
                piece = ib.at[r, hi, (y + d) % 4, 1 - core, lo]
                arrive(piece, base + C_AG + d * 8 + k, sib)

    def scatter_items_core(r):
        base = r * PER_ROUND
        for d in (2, 1, 3, 0):
            other = (y + d) % 4
            send(pi.at[r, :, other, 1 - core], rc.at[r, :, other], base + C_RS + d, sib)

    def scatter_items_y(r):
        base = r * PER_ROUND
        for d in (2, 1, 3, 0):
            other = (y + d) % 4
            arrive(rc.at[r, :, other], base + C_RS + d, sib)
            sums = pi[r, :, other, core] + rc[r, :, other]
            hb[r, other] = sums.reshape(8, 16, 256)
        for k in FAR_FIRST + (0,):
            at = (z + k) % 8
            for d in (2, 1, 3):
                source = hb.at[r, (y + d) % 4, at]
                send(source, yb[d - 1].at[r, at], base + Y_RS + (d - 1) * 8 + k, y_dev(d))

    def scatter_items_z(r, steps):
        base = r * PER_ROUND
        for k in steps:
            at = (z + k) % 8
            total = hb[r, y, at]
            for d in range(1, 4):
                arrive(yb[d - 1].at[r, at], base + Y_RS + (d - 1) * 8 + k, y_dev(d))
                total = total + yb[d - 1][r, at]
            zs[r, at] = total
            if k:
                send(zs.at[r, at], zb.at[r, k - 1], base + Z_RS + k - 1, z_dev(k)[0])

    def scatter_items_total(r):
        base = r * PER_ROUND
        total = zs[r, z]
        for k in NEAR_FIRST:
            arrive(zb.at[r, k - 1], base + Z_RS + k - 1, z_dev(8 - k)[0])
            total = total + zb[r, k - 1]
        return total

    def store_items(r, m, value):
        first = 2 * m % 4
        pi[r, m // 2, first : first + 2] = value.reshape(2, 2, 64, 256)

    def scatter(r):
        if r:
            scatter_users_forward(r, 0)
        scatter_items_y(r)
        scatter_users_forward(r, 1)
        if r == 0:
            to_scalars.wait()
            place_tiles(0)
        scatter_items_z(r, FAR_FIRST[:3])
        if r:
            scatter_users_sum(r, 0)
        scatter_items_z(r, FAR_FIRST[3:] + (0,))
        if r == 0:
            send_tiles(EARLY, MIDDLE)
        users = scatter_users_total(r)
        if r:
            users = gu[...] + users
        else:
            gu[...] = users
        if r < LAYERS:
            gather_users_start(r + 1, users)
        items = scatter_items_total(r)
        if r:
            items = gi[...] + items
        else:
            gi[...] = items
        return users, items

    def send_tiles(first, last):
        for n in range(first, last):
            h = n // 6
            start = (2 * h + 1 - c % 2) * GROUP + n % 6 * PIECE
            send(
                tiles_ref.at[pl.ds(start, PIECE)],
                tbuf[h].at[1, pl.ds(n % 6 * PIECE, PIECE)],
                TILES + n,
                pair_dev,
            )

    def place_tiles(h):
        own_tiles[h].wait()
        for n in range(6 * h, 6 * h + 6):
            arrive(tbuf[h].at[1, pl.ds(n % 6 * PIECE, PIECE)], TILES + n, pair_dev)

        def place(row, carry):
            at_row = pl.ds(pl.multiple_of(h * 512 + row * 128, 128), 128)
            for col in range(8):
                at_col = slice(col * 128, (col + 1) * 128)
                spot = (2 * h + c % 2) * PLACES + row * 8 + col
                tile = tbuf[h][0, sints[0, 0, spot]] + tbuf[h][1, sints[1, 0, spot]]
                ah[at_row, at_col], al[at_row, at_col] = split2(tile)
                ath[at_col, at_row], atl[at_col, at_row] = split2(tile.T)
            return carry

        lax.fori_loop(0, 4, place, 0)

    to_scalars = pltpu.make_async_copy(gsource, sints, lsem.at[2])

    def loss_gradient():
        for k in range(1, 4):
            dev, other = hot_dev(k)
            send(gints.at[0], gints.at[k], INTS + k - 1, dev)
        send(gsource.at[0], gsource.at[1], SOURCE, pair_dev)
        gather_items_start(0, None)
        gather_users_start(0, None)
        send_tiles(0, EARLY)
        gather_items_z(0, NEAR_FIRST[:2])
        gather_users_forward(0)
        for k in range(1, 4):
            arrive(gints.at[k], INTS + k - 1, hot_dev(4 - k)[0])
        arrive(gsource.at[1], SOURCE, pair_dev)
        to_scalars.start()
        gather_items_z(0, NEAR_FIRST[2:])
        for k in range(1, 4):
            select_users(k)
        gather_items_y(0, (0,) + NEAR_FIRST[:4])
        for k in range(1, 4):
            select_items(k)
        gather_items_y(0, NEAR_FIRST[4:])
        gather_users_end(0)
        ut[0], ut[1], ut[2] = split3(ub[0, slot].reshape(512, 256))
        for h in range(4):
            span = slice(h * 256, (h + 1) * 256)
            hot = uho[span]
            buy[span] = dot(hot, ut[0]) + dot(hot, ut[1]) + dot(hot, ut[2])
        gather_items_end(0)
        dt[0], dt[1], dt[2] = split3(ib[0].reshape(1024, 256))
        for h in range(4):
            span = slice(h * 256, (h + 1) * 256)
            buyer, signed = buy[span], dho[span]
            differ = dot(signed, dt[0]) + dot(signed, dt[1]) + dot(signed, dt[2])
            margin = jnp.sum(buyer * differ, axis=1, keepdims=True)
            small = jnp.exp(-jnp.abs(margin))
            coef = -jnp.where(margin >= 0, small, 1.0) / (1.0 + small)
            wu[0, span], wu[1, span] = split2(coef * buyer)
            wd[0, span], wd[1, span] = split2(coef * differ)
        for m in range(4):
            left = ohd[m * 256 : (m + 1) * 256, :]
            store_items(0, m, dot(left, wu[0]) + dot(left, wu[1]))
        scatter_items_core(0)
        sums = dot(ohu[...], wd[0]) + dot(ohu[...], wd[1])
        pu[0, slot] = sums.reshape(4, 128, 256)
        scatter_users_start(0, 1)
        return scatter(0)

    def layer(r, items):
        gather_items_start(r, items)
        gather_users_over_z(r)
        if r == 1:
            send_tiles(MIDDLE, PIECES)
        gather_items_z(r, NEAR_FIRST[:2])
        gather_users_forward(r)
        gather_items_z(r, NEAR_FIRST[2:6])
        gather_users_far(r, (0, 1))
        gather_items_z(r, NEAR_FIRST[6:])
        gather_items_y(r, (0,) + NEAR_FIRST[:4])
        gather_users_far(r, (2, 3))
        if r == 1:
            place_tiles(1)
        gather_items_y(r, NEAR_FIRST[4:])
        gather_items_end(r)
        xh, xl = split2(ib[r].reshape(1024, 256))
        for own in range(2):
            place = place_of(own)
            rows = pl.ds(pl.multiple_of(place * 512, 512), 512)
            sums = dot(ah[rows], xh) + dot(ah[rows], xl) + dot(al[rows], xh)
            pu[r, place] = sums.reshape(4, 128, 256)
            scatter_users_start(r, own)
        gather_users_end(r)
        uh, ul = split2(ub[r].reshape(1024, 256))
        for m in range(4):
            rows = slice(m * 256, (m + 1) * 256)
            store_items(r, m, dot(ath[rows], uh) + dot(ath[rows], ul) + dot(atl[rows], uh))
        scatter_items_core(r)
        return scatter(r)

    def rounds():
        users, items = loss_gradient()
        for r in range(1, ROUNDS):
            users, items = layer(r, items)
        return users, items

    users, items = rounds()
    uo_ref[...] = users / (LAYERS + 1.0)
    io_ref[...] = items / (LAYERS + 1.0)
    for copy in started:
        copy.wait_send()


def body(user_final, item_final, tiles, tile_rows, tile_cols, tile_count, triplets):
    slot = jnp.arange(4 * GROUP, dtype=jnp.int32)
    spot = slot // GROUP * PLACES + tile_rows // 4 * 8 + tile_cols
    spot = jnp.where(slot < tile_count[0], spot, -1)
    vmem = pl.BlockSpec(memory_space=pltpu.VMEM)
    smem = pl.BlockSpec(memory_space=pltpu.SMEM)
    hbm = pl.BlockSpec(memory_space=pltpu.HBM)
    return pl.pallas_call(
        kernel,
        out_shape=(
            jax.ShapeDtypeStruct((128, 256), F32),
            jax.ShapeDtypeStruct((16, 256), F32),
        ),
        in_specs=[vmem, smem, hbm, hbm, hbm],
        out_specs=(vmem, vmem),
        scratch_shapes=[
            pltpu.VMEM((4, 8, 256), jnp.int32),
            pltpu.VMEM((2, 1, 128), jnp.int32),
            pltpu.SMEM((2, 1, 128), jnp.int32),
            pltpu.VMEM((2, GROUP + 1, 128, 128), F32),
            pltpu.VMEM((2, GROUP + 1, 128, 128), F32),
            pltpu.VMEM((1024, 1024), BF16),
            pltpu.VMEM((1024, 1024), BF16),
            pltpu.VMEM((1024, 1024), BF16),
            pltpu.VMEM((1024, 1024), BF16),
            pltpu.VMEM((512, 1024), BF16),
            pltpu.VMEM((1024, 1024), BF16),
            pltpu.VMEM((1024, 512), BF16),
            pltpu.VMEM((1024, 1024), BF16),
            pltpu.VMEM((1024, 256), F32),
            pltpu.VMEM((3, 512, 256), BF16),
            pltpu.VMEM((3, 1024, 256), BF16),
            pltpu.VMEM((2, 1024, 256), BF16),
            pltpu.VMEM((2, 1024, 256), BF16),
            pltpu.VMEM((ROUNDS, 2, 4, 128, 256), F32),
            pltpu.VMEM((ROUNDS, 2, 4, 2, 4, 16, 256), F32),
            pltpu.VMEM((ROUNDS, 2, 4, 128, 256), F32),
            pltpu.VMEM((ROUNDS, 2, 4, 2, 64, 256), F32),
            pltpu.VMEM((ROUNDS, 2, 128, 256), F32),
            pltpu.VMEM((ROUNDS, 2, 128, 256), F32),
            pltpu.VMEM((ROUNDS, 2, 128, 256), F32),
            pltpu.VMEM((ROUNDS, 128, 256), F32),
            pltpu.VMEM((ROUNDS, 2, 4, 64, 256), F32),
            pltpu.VMEM((ROUNDS, 4, 8, 16, 256), F32),
            pltpu.VMEM((ROUNDS, 8, 16, 256), F32),
            pltpu.VMEM((ROUNDS, 8, 16, 256), F32),
            pltpu.VMEM((ROUNDS, 8, 16, 256), F32),
            pltpu.VMEM((ROUNDS, 8, 16, 256), F32),
            pltpu.VMEM((ROUNDS, 7, 16, 256), F32),
            pltpu.VMEM((128, 256), F32),
            pltpu.VMEM((16, 256), F32),
            pltpu.SemaphoreType.DMA((COPIES,)),
            pltpu.SemaphoreType.DMA((COPIES,)),
            pltpu.SemaphoreType.DMA((6,)),
        ],
        compiler_params=pltpu.CompilerParams(
            collective_id=0, has_side_effects=True, vmem_limit_bytes=52 * 1024 * 1024
        ),
        name="propagate",
    )(triplets.T, spot, user_final, item_final, tiles)


def solution(mesh):
    placed = (
        P(("user", "item", "hot"), None),
        P(("user", "item", "hot"), None),
        P(("user", "item", "hot"), None, None),
        P(("user", "item", "hot")),
        P(("user", "item", "hot")),
        P(("user", "item", "hot")),
        P(("user", "item", "hot"), None),
    )
    return jax.shard_map(
        body,
        mesh=mesh,
        in_specs=placed,
        out_specs=(P(("user", "item", "hot"), None), P(("user", "item", "hot"), None)),
        check_vma=False,
    )
```
